32 devices in a mesh: shard: 2 (over y), ctx: 4 (over z), tp: 4 (over x, core).
Axes of the slice: x: 2, y: 2, z: 4, core: 2. Of those that a mesh axis runs over, the one named last changes fastest.
Arguments:
- hidden_in: bfloat16 [4, 1024, 2560], P('shard', 'ctx'), may hold values from -6 to 6
- cotangent: bfloat16 [4, 1024, 2560], P('shard', 'ctx'), may hold values from -6 to 6
- doc_lengths: int32 [4, 4], P('shard'), may hold values from 1 to 896, as said below
- attn_gain: bfloat16 [2560], P(('shard', 'ctx', 'tp')), may hold values from 0.5 to 1.5
- q_gain: bfloat16 [768], P(('shard', 'ctx', 'tp')), may hold values from 0.5 to 1.5
- kv_gain: bfloat16 [256], P(('shard', 'ctx', 'tp')), may hold values from 0.5 to 1.5
- ffn_gain: bfloat16 [2560], P(('shard', 'ctx', 'tp')), may hold values from 0.5 to 1.5
- q_down: bfloat16 [2560, 768], P(('shard', 'ctx', 'tp')), may hold values from -0.125 to 0.125
- kv_down: bfloat16 [2560, 288], P(('shard', 'ctx', 'tp')), may hold values from -0.125 to 0.125
- q_up: bfloat16 [768, 3840], P(('shard', 'ctx'), 'tp'), may hold values from -0.4375 to 0.4375
- kv_up: bfloat16 [256, 5120], P(('shard', 'ctx'), 'tp'), may hold values from -0.375 to 0.375
- out_proj: bfloat16 [2560, 2560], P('tp', ('shard', 'ctx')), may hold values from -3 to 3
- gate_proj: bfloat16 [2560, 6400], P(('shard', 'ctx'), 'tp'), may hold values from -0.125 to 0.125
- up_proj: bfloat16 [2560, 6400], P(('shard', 'ctx'), 'tp'), may hold values from -0.125 to 0.125
- down_proj: bfloat16 [6400, 2560], P('tp', ('shard', 'ctx')), may hold values from -0.75 to 0.75
Outputs:
- output: float32 [4, 1024, 2560], P('shard', 'ctx')
- grad_input: float32 [4, 1024, 2560], P('shard', 'ctx')
- grad_attn_gain: float32 [2560], P(('shard', 'ctx', 'tp'))
- grad_q_gain: float32 [768], P(('shard', 'ctx', 'tp'))
- grad_kv_gain: float32 [256], P(('shard', 'ctx', 'tp'))
- grad_ffn_gain: float32 [2560], P(('shard', 'ctx', 'tp'))
- grad_q_down: float32 [2560, 768], P(('shard', 'ctx', 'tp'))
- grad_kv_down: float32 [2560, 288], P(('shard', 'ctx', 'tp'))
- grad_q_up: float32 [768, 3840], P(('shard', 'ctx'), 'tp')
- grad_kv_up: float32 [256, 5120], P(('shard', 'ctx'), 'tp')
- grad_out_proj: float32 [2560, 2560], P('tp', ('shard', 'ctx'))
- grad_gate_proj: float32 [2560, 6400], P(('shard', 'ctx'), 'tp')
- grad_up_proj: float32 [2560, 6400], P(('shard', 'ctx'), 'tp')
- grad_down_proj: float32 [6400, 2560], P('tp', ('shard', 'ctx'))
The draws below stay inside these ranges and needn't reach their ends.
Inputs may be any that keep to these rules, and one draw needn't show every extreme that they name: `doc_lengths`: in every sequence the 4 lengths are positive and sum to 1024; exactly one of them, at a place drawn for each sequence, is 896.
All inputs are finite; a program needn't handle non-finite values.
Results may differ from the reference program's by a relative error of at most 0.02.
Values may be sent and summed in bfloat16 or wider, within the bound.
No kernel may reach another device: no remote copies, remote signals or barrier semaphores. Data moves between devices by JAX's collectives and lax.ppermute only.
A program may use at most 320 MiB of HBM per device.

```python
import math
import jax
import jax.numpy as jnp
from jax import lax

D = 2560
HEADS = 40
NOPE = 64
ROPE = 32
VDIM = 64
QRANK = 768
KVRANK = 256
FF = 6400
LEN = 1024
DOCS = 4
SEQS = 4
LONG_DOC = 896


def draw_doc_lengths(key, part):
    short_total = LEN - LONG_DOC
    key_cut = jax.random.fold_in(key, 11)
    key_place = jax.random.fold_in(key, 12)
    ranks = jax.random.randint(key_cut, (SEQS, short_total - 1), 0, 1 << 20) * (short_total - 1)
    ranks = ranks + jnp.arange(short_total - 1, dtype=jnp.int32)[None, :]
    chosen = jnp.argsort(ranks, axis=1)[:, :DOCS - 2].astype(jnp.int32) + 1
    cuts = jnp.sort(chosen, axis=1)
    bounds = jnp.concatenate([jnp.zeros((SEQS, 1), jnp.int32), cuts, jnp.full((SEQS, 1), short_total, jnp.int32)], axis=1)
    pieces = bounds[:, 1:] - bounds[:, :-1]
    place = jax.random.randint(key_place, (SEQS, 1), 0, DOCS)
    slots = jnp.arange(DOCS, dtype=jnp.int32)[None, :]
    source = jnp.clip(slots - (slots > place).astype(jnp.int32), 0, DOCS - 2)
    taken = jnp.take_along_axis(pieces, source, axis=1)
    return jnp.where(slots == place, LONG_DOC, taken).astype(jnp.int32)


def block_levels(rng, extent, cuts, low, high):
    loudness, own = 1.0, jax.random.fold_in(rng, 6)
    for dim, parts in cuts:
        draws = jnp.exp(jax.random.uniform(jax.random.fold_in(own, dim), (parts,), jnp.float32, low / len(cuts), high / len(cuts)))
        loudness = loudness * jnp.repeat(draws, extent[dim] // parts).reshape([-1 if axis == dim else 1 for axis in range(len(extent))])
    return loudness


def centred(own_key, extent, scale, reach, split=(), held_as=jnp.bfloat16):
    result = jax.random.normal(own_key, extent, jnp.float32) * scale
    if len(split) > 0:
        result = block_levels(own_key, extent, split, -0.22, 0.18) * result
    return jnp.clip(result, min=-reach, max=reach).astype(held_as)


def setup_inputs(seed: int = 0) -> dict:
    keys = jax.random.split(jax.random.key(seed), 16)
    return {
        "hidden_in": centred(keys[0], (SEQS, LEN, D), 1.0, 6.0, ((0, 2), (1, 4))),
        "cotangent": centred(keys[1], (SEQS, LEN, D), 1.0, 6.0, ((0, 2), (1, 4))),
        "doc_lengths": draw_doc_lengths(jax.random.fold_in(keys[15], 71), 0),
        "attn_gain": jnp.clip(1.0 + 0.1 * jax.random.normal(keys[3], (D,), jnp.float32), 0.5, 1.5).astype(jnp.bfloat16),
        "q_gain": jnp.clip(1.0 + 0.1 * jax.random.normal(keys[4], (QRANK,), jnp.float32), 0.5, 1.5).astype(jnp.bfloat16),
        "kv_gain": jnp.clip(1.0 + 0.1 * jax.random.normal(keys[5], (KVRANK,), jnp.float32), 0.5, 1.5).astype(jnp.bfloat16),
        "ffn_gain": jnp.clip(1.0 + 0.1 * jax.random.normal(keys[6], (D,), jnp.float32), 0.5, 1.5).astype(jnp.bfloat16),
        "q_down": centred(keys[7], (D, QRANK), D ** -0.5, 0.125, ((0, 32),)),
        "kv_down": centred(keys[8], (D, KVRANK + ROPE), D ** -0.5, 0.125, ((0, 32),)),
        "q_up": centred(keys[9], (QRANK, HEADS * (NOPE + ROPE)), (QRANK // 4) ** -0.5, 0.4375, ((0, 8), (1, 4))),
        "kv_up": centred(keys[10], (KVRANK, HEADS * (NOPE + VDIM)), KVRANK ** -0.5, 0.375, ((0, 8), (1, 4))),
        "out_proj": centred(keys[11], (HEADS * VDIM, D), 4 ** -0.5, 3.0, ((0, 4), (1, 8))),
        "gate_proj": centred(keys[12], (D, FF), D ** -0.5, 0.125, ((0, 8), (1, 4))),
        "up_proj": centred(keys[13], (D, FF), D ** -0.5, 0.125, ((0, 8), (1, 4))),
        "down_proj": centred(keys[14], (FF, D), 64 ** -0.5, 0.75, ((0, 4), (1, 8))),
    }


@jax.custom_vjp
def low(v):
    return lax.optimization_barrier(v.astype(jnp.bfloat16)).astype(jnp.float32)

@jax.custom_vjp
def low_back(v):
    return v

def low_keep(v):
    return (low(v), None)

def low_pass(kept, grad):
    return (grad,)

def back_keep(v):
    return (v, None)

def back_low(kept, grad):
    return (low(grad),)
low.defvjp(low_keep, low_pass)
low_back.defvjp(back_keep, back_low)
eps = 1e-05
res_scale = 1.4 / math.sqrt(62.0)
big_negative = -1e+30
highest = lax.Precision.HIGHEST

def matmul(left, right):
    return jnp.dot(left, right, precision=highest)

def rms_norm(values, gain):
    return values * lax.rsqrt(lax.optimization_barrier(jnp.mean(values * values, axis=-1, keepdims=True)) + eps) * gain

def rope_tables(positions):
    half = ROPE // 2
    inverse = jnp.exp(-math.log(10000.0) * jnp.arange(half).astype(jnp.float32) * 2.0 / ROPE)
    angles = positions.astype(jnp.float32)[:, None] * inverse[None, :]
    angles = jnp.concatenate([angles, angles], axis=-1)
    return (jnp.cos(angles), jnp.sin(angles))

def rotate_half(values):
    half = values.shape[-1] // 2
    return jnp.concatenate([-values[..., half:], values[..., :half]], axis=-1)

def rotate(values, cosine, sine):
    return values * cosine + rotate_half(values) * sine

def layer_one(stream, lengths, params):
    gain_attn, gain_query, gain_latent, gain_ffn, down_query, down_latent, up_query, up_latent, out_weight, gate_weight, upward_weight, down_weight = params
    scale = 1.0 / math.sqrt(NOPE + ROPE)
    positions = jnp.arange(LEN).astype(jnp.int32)
    doc_ends = jnp.cumsum(lengths)
    segment = lax.optimization_barrier(jnp.sum((positions[:, None] >= doc_ends[None, :]).astype(jnp.int32), axis=-1))
    allowed = (positions[:, None] >= positions[None, :]) & (segment[:, None] == segment[None, :])
    cosine, sine = rope_tables(positions)
    input_low = low(rms_norm(stream, gain_attn))
    query_low = low(rms_norm(matmul(input_low, down_query), gain_query))
    latent_raw = matmul(input_low, down_latent)
    latent_low = low(rms_norm(latent_raw[:, :KVRANK], gain_latent))
    rotary_key = low(rotate(latent_raw[:, KVRANK:], cosine, sine))
    query = low_back(matmul(query_low, up_query)).reshape(LEN, HEADS, NOPE + ROPE)
    query_nope = low(query[..., :NOPE])
    query_rope = low(rotate(query[..., NOPE:], cosine[:, None, :], sine[:, None, :]))
    key_value = matmul(latent_low, up_latent).reshape(LEN, HEADS, NOPE + VDIM)
    key_nope = low(key_value[..., :NOPE])
    value_low = low(key_value[..., NOPE:])
    scores = jnp.einsum('qhd,khd->hqk', query_nope, key_nope, precision=highest)
    scores = scores + jnp.einsum('qhd,kd->hqk', query_rope, rotary_key, precision=highest)
    scores = jnp.where(allowed[None], low_back(scores * scale), big_negative)
    row_max = lax.optimization_barrier(jnp.max(scores, axis=-1, keepdims=True))
    weights = jnp.exp(scores - row_max)
    prob_low = low(weights / lax.optimization_barrier(jnp.sum(weights, axis=-1, keepdims=True)))
    attended = jnp.einsum('hqk,khd->qhd', prob_low, value_low, precision=highest)
    attended = low(low_back(attended)).reshape(LEN, HEADS * VDIM)
    middle = stream + res_scale * low_back(matmul(attended, out_weight))
    ffn_low = low(rms_norm(middle, gain_ffn))
    gate_value = low_back(matmul(ffn_low, gate_weight))
    up_value = low_back(matmul(ffn_low, upward_weight))
    hidden_low = low(jax.nn.silu(gate_value) * up_value)
    return middle + res_scale * low_back(matmul(hidden_low, down_weight))

def reference(hidden_in, cotangent, doc_lengths, attn_gain, q_gain, kv_gain, ffn_gain, q_down, kv_down, q_up, kv_up, out_proj, gate_proj, up_proj, down_proj):
    params = (attn_gain.astype(jnp.float32), q_gain.astype(jnp.float32), kv_gain.astype(jnp.float32), ffn_gain.astype(jnp.float32), q_down.astype(jnp.float32), kv_down.astype(jnp.float32), q_up.astype(jnp.float32), kv_up.astype(jnp.float32), out_proj.astype(jnp.float32), gate_proj.astype(jnp.float32), up_proj.astype(jnp.float32), down_proj.astype(jnp.float32))
    stream = hidden_in.astype(jnp.float32)

    def forward(stream_all, weights_all):

        def step(carry, item):
            return (carry, jax.checkpoint(layer_one)(item[0], item[1], weights_all))
        return lax.scan(step, None, (stream_all, doc_lengths))[1]
    output, pullback = jax.vjp(forward, stream, params)
    grad_input, grads = pullback(cotangent.astype(jnp.float32))
    return (output, grad_input, grads[0], grads[1], grads[2], grads[3], grads[4], grads[5], grads[6], grads[7], grads[8], grads[9], grads[10], grads[11])
```

```python
import math

import jax
import jax.numpy as jnp
from jax import lax
from jax.sharding import PartitionSpec as P

NOPE = 64
ROPE = 32
VDIM = 64
KVRANK = 256
QRANK = 768
PAD = 16

eps = 1e-05
res_scale = 1.4 / math.sqrt(62.0)
big_negative = -1e30
f32 = jnp.float32
bf16 = jnp.bfloat16


def rope_tables(positions):
    half = ROPE // 2
    inverse = jnp.exp(-math.log(10000.0) * jnp.arange(half, dtype=f32) * 2.0 / ROPE)
    angles = positions.astype(f32)[:, None] * inverse[None, :]
    angles = jnp.concatenate([angles, angles], axis=-1)
    return (jnp.cos(angles), jnp.sin(angles))


def rotate_half(values):
    half = values.shape[-1] // 2
    return jnp.concatenate([-values[..., half:], values[..., :half]], axis=-1)


def rotate(values, cosine, sine):
    return values * cosine + rotate_half(values) * sine


def unrotate(grads, cosine, sine):
    return grads * cosine - rotate_half(grads) * sine


def rms_inverse(values):
    return lax.rsqrt(jnp.mean(values * values, axis=-1, keepdims=True) + eps)


def norm_backward(grad_out, normed, inverse_rms, gain):
    scaled = grad_out * gain
    return inverse_rms * (scaled - normed * jnp.mean(scaled * normed, axis=-1, keepdims=True))


def dot(left, right, dims):
    return lax.dot_general(left, right, (dims, ((), ())), preferred_element_type=f32)


def round_low(values):
    return lax.reduce_precision(values, 8, 7)


def tp_xor(values, mask):
    size = lax.axis_size("tp")
    return lax.ppermute(values, "tp", [(i, i ^ mask) for i in range(size)])


def from_ctx(values, shift):
    size = lax.axis_size("ctx")
    return lax.ppermute(values, "ctx", [((i + shift) % size, i) for i in range(size)])


def gather_ctx(values):
    size = lax.axis_size("ctx")
    spread = jnp.broadcast_to(values[None], (size,) + values.shape)
    return lax.all_to_all(spread, "ctx", 0, 0)


def pair_order(own, other, second, axis):
    return jnp.concatenate(
        [jnp.where(second, other, own), jnp.where(second, own, other)], axis=axis
    )


def gather_shard(values, axis):
    if lax.axis_size("shard") == 2:
        other = lax.ppermute(values, "shard", [(0, 1), (1, 0)])
        return pair_order(values, other, lax.axis_index("shard") == 1, axis)
    return lax.all_gather(values, "shard", axis=axis, tiled=True)


def scatter_shard(values, axis):
    size = lax.axis_size("shard")
    if size == 2:
        length = values.shape[axis] // 2
        low = lax.slice_in_dim(values, 0, length, axis=axis)
        high = lax.slice_in_dim(values, length, 2 * length, axis=axis)
        second = lax.axis_index("shard") == 1
        keep = jnp.where(second, high, low)
        send = jnp.where(second, low, high).astype(bf16)
        return keep + lax.ppermute(send, "shard", [(0, 1), (1, 0)]).astype(f32)
    return lax.psum_scatter(
        values.astype(bf16), "shard", scatter_dimension=axis, tiled=True
    ).astype(f32)


def scatter_ctx(values):
    came = lax.all_to_all(values.astype(bf16), "ctx", 0, 0)
    return jnp.sum(came.astype(f32), axis=0)


def gather_tp(chunk):
    rank = lax.axis_index("tp")
    low_bit, high_bit = (rank & 1) == 1, (rank >> 1) == 1
    other = tp_xor(chunk, 2)
    pair = jnp.stack([jnp.where(high_bit, other, chunk), jnp.where(high_bit, chunk, other)])
    across = tp_xor(pair, 1)
    both = jnp.stack(
        [jnp.where(low_bit, across, pair), jnp.where(low_bit, pair, across)], axis=1
    )
    return both.reshape((4,) + chunk.shape)


def scatter_tp(partial_sum):
    rank = lax.axis_index("tp")
    low_bit, high_bit = (rank & 1) == 1, (rank >> 1) == 1
    parts = partial_sum.reshape((2, 2) + partial_sum.shape[1:])
    keep = jnp.where(low_bit, parts[:, 1], parts[:, 0])
    send = jnp.where(low_bit, parts[:, 0], parts[:, 1]).astype(bf16)
    summed = keep + tp_xor(send, 1).astype(f32)
    keep = jnp.where(high_bit, summed[1], summed[0])
    send = jnp.where(high_bit, summed[0], summed[1]).astype(bf16)
    return keep + tp_xor(send, 2).astype(f32)


def gather_tokens(chunk, own):
    groups = []
    for shift in range(lax.axis_size("ctx")):
        if shift == 0 and own is not None:
            groups.append(own)
            continue
        here = from_ctx(chunk, shift) if shift else chunk
        far = tp_xor(here, 2)
        near, near_far = tp_xor(here, 1), tp_xor(far, 1)
        groups.append(jnp.concatenate([here, near, far, near_far], axis=0))
    return groups


def scatter_tokens(partial_sums):
    size = lax.axis_size("ctx")
    total = None
    for shift in reversed(range(size)):
        parts = partial_sums[shift].reshape((4, -1, partial_sums[shift].shape[-1]))
        came = tp_xor(jnp.stack([parts[1], parts[3]]).astype(bf16), 1).astype(f32)
        near, far = parts[0] + came[0], parts[2] + came[1]
        summed = near + tp_xor(far.astype(bf16), 2).astype(f32)
        if shift:
            summed = lax.ppermute(
                summed.astype(bf16), "ctx", [(i, (i + shift) % size) for i in range(size)]
            ).astype(f32)
        total = summed if total is None else total + summed
    return total


def on_device(
    hidden_in,
    cotangent,
    doc_lengths,
    attn_gain,
    q_gain,
    kv_gain,
    ffn_gain,
    q_down,
    kv_down,
    q_up,
    kv_up,
    out_proj,
    gate_proj,
    up_proj,
    down_proj,
):
    seqs, piece, width = hidden_in.shape
    n_shard, n_ctx, n_tp = lax.axis_size("shard"), lax.axis_size("ctx"), lax.axis_size("tp")
    rank = lax.axis_index("tp")
    low_bit = (rank & 1) == 1
    rows = seqs * piece
    chunk_rows = rows // n_tp
    seq_len = piece * n_ctx
    offset = lax.axis_index("ctx") * piece
    scale = 1.0 / math.sqrt(NOPE + ROPE)
    q_part, kv_part = QRANK // n_tp, (KVRANK + ROPE) // n_tp
    part = q_part + kv_part
    block = q_down.shape[0]
    n_gain = 2 * attn_gain.shape[0] + q_gain.shape[0] + kv_gain.shape[0]

    gain_row = jnp.concatenate([attn_gain, ffn_gain, q_gain, kv_gain])
    gain_rows = jnp.pad(gain_row[None], ((0, PAD - 1), (0, part - n_gain)))
    small = jnp.stack(
        [
            jnp.concatenate(
                [
                    jnp.concatenate(
                        [
                            q_down[:, i * q_part : (i + 1) * q_part],
                            kv_down[:, i * kv_part : (i + 1) * kv_part],
                        ],
                        axis=1,
                    ),
                    gain_rows,
                ],
                axis=0,
            )
            for i in range(n_tp)
        ]
    )
    small = lax.all_to_all(small, "tp", 0, 0)
    small = gather_shard(gather_ctx(small), 0)
    small = small.reshape(n_shard * n_ctx * n_tp, block + PAD, part)
    gains = small[:, block, :].astype(f32)
    cut = attn_gain.shape[0]
    gain_attn = gains[:, :cut].reshape(1, -1)
    gain_ffn = gains[:, cut : 2 * cut].reshape(1, -1)
    gain_query = gains[:, 2 * cut : 2 * cut + q_gain.shape[0]].reshape(1, -1)
    gain_latent = gains[:, 2 * cut + q_gain.shape[0] : n_gain].reshape(1, -1)
    down_part = small[:, :block, :].reshape(width, part)

    up_query = gather_shard(gather_ctx(q_up).reshape(-1, q_up.shape[1]), 0)
    up_latent = gather_shard(gather_ctx(kv_up).reshape(-1, kv_up.shape[1]), 0)
    out_full = gather_shard(
        gather_ctx(out_proj).transpose(1, 0, 2).reshape(out_proj.shape[0], -1), 1
    )

    gate_full = gather_shard(lax.all_to_all(gate_proj, "ctx", 1, 0, tiled=True), 0)
    upward_full = gather_shard(lax.all_to_all(up_proj, "ctx", 1, 0, tiled=True), 0)
    down_full = gather_shard(lax.all_to_all(down_proj, "ctx", 0, 1, tiled=True), 1)

    down_all = gather_tp(down_part)
    down_query = down_all[:, :, :q_part].transpose(1, 0, 2).reshape(width, QRANK)
    down_latent = down_all[:, :, q_part:].transpose(1, 0, 2).reshape(width, KVRANK + ROPE)

    heads = up_query.shape[1] // (NOPE + ROPE)
    positions_all = jnp.arange(seq_len, dtype=jnp.int32)
    positions_here = offset + jnp.arange(piece, dtype=jnp.int32)
    cosine_here, sine_here = rope_tables(positions_here)
    ends = jnp.stack(
        [jnp.sum(doc_lengths[:, : i + 1], axis=1) for i in range(doc_lengths.shape[1])], axis=1
    )

    def segments(positions):
        return jnp.sum((positions[None, :, None] >= ends[:, None, :]).astype(jnp.int32), axis=-1)

    segment_all, segment_here = segments(positions_all), segments(positions_here)
    causal = positions_here[:, None] >= positions_all[None, :]
    allowed = (causal[None] & (segment_here[:, :, None] == segment_all[:, None, :]))[:, None]

    stream = hidden_in.astype(f32).reshape(rows, width)
    grad_out = cotangent.astype(f32).reshape(rows, width)
    chunk_start = rank * chunk_rows

    def own_chunk(values):
        return lax.dynamic_slice_in_dim(values, chunk_start, chunk_rows, 0)

    def rank_groups(values):
        grouped = values.reshape(n_tp, chunk_rows, values.shape[-1])
        return jnp.concatenate(
            [lax.dynamic_index_in_dim(grouped, rank ^ i, 0, False) for i in range(n_tp)], axis=0
        )

    grad_ffn = (res_scale * grad_out).astype(bf16)
    grad_ffn_groups = gather_tokens(own_chunk(grad_ffn), rank_groups(grad_ffn))

    inverse_one = rms_inverse(stream)
    normed_one = stream * inverse_one
    input_low = (normed_one * gain_attn).astype(bf16)
    low_rank = gather_tp(dot(input_low, down_part, ((1,), (0,))))
    query_latent = low_rank[:, :, :q_part].transpose(1, 0, 2).reshape(rows, QRANK)
    latent_raw = low_rank[:, :, q_part:].transpose(1, 0, 2).reshape(rows, KVRANK + ROPE)
    inverse_latent = rms_inverse(latent_raw[:, :KVRANK])
    normed_latent = latent_raw[:, :KVRANK] * inverse_latent
    latent_low = (normed_latent * gain_latent).astype(bf16).reshape(seqs, piece, KVRANK)
    rotary_key = rotate(
        latent_raw[:, KVRANK:].reshape(seqs, piece, ROPE), cosine_here, sine_here
    ).astype(bf16)
    keys_here = jnp.concatenate([latent_low, rotary_key], axis=-1)
    keys_half = keys_here.reshape(seqs, 2, piece // 2, KVRANK + ROPE)
    keys_half = gather_ctx(jnp.where(low_bit, keys_half[:, 1], keys_half[:, 0]))
    keys_other = tp_xor(keys_half, 1)
    keys_all = jnp.stack(
        [
            jnp.where(low_bit, keys_other, keys_half),
            jnp.where(low_bit, keys_half, keys_other),
        ],
        axis=2,
    )
    keys_all = keys_all.transpose(1, 0, 2, 3, 4).reshape(seqs, seq_len, KVRANK + ROPE)
    latent_all, rotary_all = keys_all[..., :KVRANK], keys_all[..., KVRANK:]

    inverse_query = rms_inverse(query_latent)
    normed_query = query_latent * inverse_query
    query_low = (normed_query * gain_query).astype(bf16)
    key_value = jnp.einsum("slr,rf->slf", latent_all, up_latent, preferred_element_type=f32)
    key_value = key_value.reshape(seqs, seq_len, heads, NOPE + VDIM)
    key_nope = key_value[..., :NOPE].astype(bf16)
    value_low = key_value[..., NOPE:].astype(bf16)
    query = dot(query_low, up_query, ((1,), (0,))).reshape(seqs, piece, heads, NOPE + ROPE)
    query_nope = query[..., :NOPE].astype(bf16)
    query_rope = rotate(query[..., NOPE:], cosine_here[:, None, :], sine_here[:, None, :]).astype(
        bf16
    )

    def masked_scores():
        raw = jnp.einsum("sqhd,skhd->shqk", query_nope, key_nope, preferred_element_type=f32)
        raw = raw + jnp.einsum("sqhd,skd->shqk", query_rope, rotary_all, preferred_element_type=f32)
        return jnp.where(allowed, raw * scale, big_negative)

    scores = masked_scores()
    row_max = jnp.max(scores, axis=-1, keepdims=True)
    weights = jnp.exp(scores - row_max)
    row_total = jnp.sum(weights, axis=-1, keepdims=True)
    log_total = row_max + jnp.log(row_total)
    prob_low = (weights / row_total).astype(bf16)
    attended = jnp.einsum("shqk,skhd->sqhd", prob_low, value_low, preferred_element_type=f32)
    attended_low = attended.reshape(rows, heads * VDIM).astype(bf16)

    attn_out = scatter_tp(
        dot(attended_low, out_full, ((1,), (0,))).reshape(n_tp, chunk_rows, width)
    )
    middle = own_chunk(stream) + res_scale * attn_out
    inverse_two = rms_inverse(middle)
    normed_two = middle * inverse_two
    ffn_groups = gather_tokens((normed_two * gain_ffn).astype(bf16), None)

    ffn_parts, grad_two_parts = [], []
    grad_gate_w = grad_upward_w = grad_down_w = 0.0
    for ffn_low, grad_low in zip(ffn_groups, grad_ffn_groups):
        gate_value = dot(ffn_low, gate_full, ((1,), (0,)))
        up_value = dot(ffn_low, upward_full, ((1,), (0,)))
        sigma = jax.nn.sigmoid(gate_value)
        gate_act = gate_value * sigma
        hidden_low = (gate_act * up_value).astype(bf16)
        grad_hidden = dot(grad_low, down_full, ((1,), (1,)))
        grad_gate = (grad_hidden * up_value * sigma * (1.0 + gate_value * (1.0 - sigma))).astype(
            bf16
        )
        grad_upward = (grad_hidden * gate_act).astype(bf16)
        grad_two_parts.append(
            dot(grad_gate, gate_full, ((1,), (1,))) + dot(grad_upward, upward_full, ((1,), (1,)))
        )
        ffn_parts.append(dot(hidden_low, down_full, ((1,), (0,))))
        grad_gate_w += dot(ffn_low, grad_gate, ((0,), (0,)))
        grad_upward_w += dot(ffn_low, grad_upward, ((0,), (0,)))
        grad_down_w += dot(hidden_low, grad_low, ((0,), (0,)))

    grad_two = scatter_tokens(grad_two_parts)
    grad_middle = own_chunk(grad_out) + norm_backward(grad_two, normed_two, inverse_two, gain_ffn)
    grad_gain_ffn = jnp.sum(grad_two * normed_two, axis=0)
    grad_attn = gather_tp((res_scale * grad_middle).astype(bf16)).reshape(rows, width)

    output = round_low(middle + res_scale * scatter_tokens(ffn_parts))
    output = gather_tp(output.astype(bf16)).astype(f32)

    grad_attended = dot(grad_attn, out_full, ((1,), (1,)))
    grad_attended = grad_attended.astype(bf16).reshape(seqs, piece, heads, VDIM)
    grad_value = jnp.einsum("shqk,sqhd->skhd", prob_low, grad_attended, preferred_element_type=f32)
    grad_prob = jnp.einsum("sqhd,skhd->shqk", grad_attended, value_low, preferred_element_type=f32)
    prob_again = jnp.exp(masked_scores() - log_total)
    grad_scores = prob_again * (grad_prob - jnp.sum(prob_again * grad_prob, axis=-1, keepdims=True))
    grad_scores = grad_scores.astype(bf16)
    grad_qnope = (
        jnp.einsum("shqk,skhd->sqhd", grad_scores, key_nope, preferred_element_type=f32) * scale
    )
    grad_qrope = (
        jnp.einsum("shqk,skd->sqhd", grad_scores, rotary_all, preferred_element_type=f32) * scale
    )
    grad_qrope = unrotate(grad_qrope, cosine_here[:, None, :], sine_here[:, None, :])
    grad_knope = (
        jnp.einsum("shqk,sqhd->skhd", grad_scores, query_nope, preferred_element_type=f32) * scale
    )
    grad_krope = (
        jnp.einsum("shqk,sqhd->skd", grad_scores, query_rope, preferred_element_type=f32) * scale
    )
    grad_query = (
        jnp.concatenate([grad_qnope, grad_qrope], axis=-1)
        .reshape(rows, heads * (NOPE + ROPE))
        .astype(bf16)
    )
    grad_key_value = jnp.concatenate([grad_knope, grad_value], axis=-1).astype(bf16)
    grad_key_value = grad_key_value.reshape(seqs * seq_len, heads * (NOPE + VDIM))

    grad_latent_all = dot(grad_key_value, up_latent, ((1,), (1,))).reshape(seqs, seq_len, KVRANK)
    grad_keys = jnp.concatenate([grad_latent_all, grad_krope], axis=-1)
    grad_keys = grad_keys.reshape(seqs, n_ctx, 2, piece // 2, KVRANK + ROPE).transpose(
        1, 2, 0, 3, 4
    )
    send = jnp.where(low_bit, grad_keys[:, 0], grad_keys[:, 1]).astype(bf16)
    grad_keys = jnp.where(low_bit, grad_keys[:, 1], grad_keys[:, 0]) + tp_xor(send, 1).astype(f32)
    grad_keys = scatter_ctx(grad_keys)
    grad_pre_query = dot(grad_query, up_query, ((1,), (1,)))
    grad_pre_query = grad_pre_query.reshape(seqs, 2, piece // 2, QRANK)
    send = jnp.where(low_bit, grad_pre_query[:, 0], grad_pre_query[:, 1]).astype(bf16)
    grad_pre_query = jnp.where(low_bit, grad_pre_query[:, 1], grad_pre_query[:, 0])
    grad_pre_query = grad_pre_query + tp_xor(send, 1).astype(f32)
    grad_low = jnp.concatenate([grad_pre_query, grad_keys], axis=-1).astype(bf16)
    grad_low = (grad_low.astype(f32) + tp_xor(grad_low, 2).astype(f32)).astype(bf16)
    grad_low = pair_order(grad_low[:, None], tp_xor(grad_low, 1)[:, None], low_bit, 1)
    grad_low = grad_low.reshape(rows, QRANK + KVRANK + ROPE).astype(f32)

    grad_out_query, grad_out_latent = grad_low[:, :QRANK], grad_low[:, QRANK : QRANK + KVRANK]
    grad_query_latent = norm_backward(grad_out_query, normed_query, inverse_query, gain_query)
    grad_compressed = norm_backward(grad_out_latent, normed_latent, inverse_latent, gain_latent)
    grad_gain_query = jnp.sum(own_chunk(grad_out_query * normed_query), axis=0)
    grad_gain_latent = jnp.sum(own_chunk(grad_out_latent * normed_latent), axis=0)
    grad_rotary = grad_low[:, QRANK + KVRANK :].reshape(seqs, piece, ROPE)
    grad_rotary = unrotate(grad_rotary, cosine_here, sine_here).reshape(rows, ROPE)
    grad_query_latent = grad_query_latent.astype(bf16)
    grad_latent_raw = jnp.concatenate([grad_compressed, grad_rotary], axis=-1).astype(bf16)

    grad_pre_one = dot(own_chunk(grad_query_latent), down_query, ((1,), (1,)))
    grad_pre_one = grad_pre_one + dot(own_chunk(grad_latent_raw), down_latent, ((1,), (1,)))
    normed_own = own_chunk(normed_one)
    grad_input = grad_middle + norm_backward(
        grad_pre_one, normed_own, own_chunk(inverse_one), gain_attn
    )
    grad_gain_attn = jnp.sum(grad_pre_one * normed_own, axis=0)
    grad_input = gather_tp(round_low(grad_input).astype(bf16)).astype(f32)

    grad_part = jnp.concatenate(
        [
            lax.dynamic_slice_in_dim(grad_query_latent, rank * q_part, q_part, 1),
            lax.dynamic_slice_in_dim(grad_latent_raw, rank * kv_part, kv_part, 1),
        ],
        axis=1,
    )
    n_blocks = n_shard * n_ctx * n_tp
    grad_small = dot(input_low, grad_part, ((0,), (0,))).reshape(n_blocks, block, part)
    grad_gains = jnp.concatenate(
        [
            grad_gain_attn.reshape(n_blocks, -1),
            grad_gain_ffn.reshape(n_blocks, -1),
            grad_gain_query.reshape(n_blocks, -1),
            grad_gain_latent.reshape(n_blocks, -1),
        ],
        axis=1,
    )
    grad_gains = jnp.pad(grad_gains[:, None], ((0, 0), (0, PAD - 1), (0, part - n_gain)))
    grad_small = jnp.concatenate([grad_small, grad_gains], axis=1)
    grad_small = scatter_ctx(
        scatter_shard(grad_small, 0).reshape(n_ctx, n_tp, block + PAD, part)
    )
    grad_small = lax.all_to_all(grad_small.astype(bf16), "tp", 0, 0).astype(f32)
    grad_gains = jnp.sum(grad_small[:, block, :], axis=0)
    grad_small = grad_small[:, :block].transpose(1, 0, 2)
    grad_down_query = grad_small[:, :, :q_part].reshape(block, QRANK)
    grad_down_latent = grad_small[:, :, q_part:].reshape(block, KVRANK + ROPE)

    def rows_grad(grad):
        mine = scatter_shard(grad, 0)
        return scatter_ctx(mine.reshape(n_ctx, -1, mine.shape[-1]))

    grad_up_query = rows_grad(dot(query_low, grad_query, ((0,), (0,))))
    grad_up_latent = rows_grad(
        dot(latent_all.reshape(-1, KVRANK), grad_key_value, ((0,), (0,)))
    )
    grad_out_w = scatter_shard(dot(attended_low, grad_attn, ((0,), (0,))), 1)
    grad_out_w = scatter_ctx(
        grad_out_w.reshape(grad_out_w.shape[0], n_ctx, -1).transpose(1, 0, 2)
    )

    def hidden_grad(grad):
        mine = scatter_shard(grad, 0).astype(bf16)
        return lax.all_to_all(mine, "ctx", 0, 1, tiled=True).astype(f32)

    grad_gate_w, grad_upward_w = hidden_grad(grad_gate_w), hidden_grad(grad_upward_w)
    grad_down_w = scatter_shard(grad_down_w, 1).astype(bf16)
    grad_down_w = lax.all_to_all(grad_down_w, "ctx", 1, 0, tiled=True).astype(f32)
    return (
        output.reshape(seqs, piece, width),
        grad_input.reshape(seqs, piece, width),
        grad_gains[:cut],
        grad_gains[2 * cut : 2 * cut + q_gain.shape[0]],
        grad_gains[2 * cut + q_gain.shape[0] : n_gain],
        grad_gains[cut : 2 * cut],
        grad_down_query,
        grad_down_latent,
        grad_up_query,
        grad_up_latent,
        grad_out_w,
        grad_gate_w,
        grad_upward_w,
        grad_down_w,
    )


def solution(mesh):
    all_axes = ("shard", "ctx", "tp")
    tokens, vector, square = P("shard", "ctx", None), P(all_axes), P(all_axes, None)
    inner, outer = P(("shard", "ctx"), "tp"), P("tp", ("shard", "ctx"))
    weights = (
        vector,
        vector,
        vector,
        vector,
        square,
        square,
        inner,
        inner,
        outer,
        inner,
        inner,
        outer,
    )
    return jax.shard_map(
        on_device,
        mesh=mesh,
        in_specs=(tokens, tokens, P("shard", None)) + weights,
        out_specs=(tokens, tokens) + weights,
        check_vma=False,
    )
```

```python
import functools
import math

import jax
import jax.numpy as jnp
from jax import lax
from jax.experimental import pallas as pl
from jax.experimental.pallas import tpu as pltpu
from jax.sharding import PartitionSpec as P

NOPE = 64
ROPE = 32
VDIM = 64
KVRANK = 256
QRANK = 768
LANES = 128
HEAD = NOPE + ROPE
score_scale = 1.0 / math.sqrt(HEAD)
log2e = 1.0 / math.log(2.0)
MIB = 1024 * 1024

eps = 1e-05
res_scale = 1.4 / math.sqrt(62.0)
big_negative = -1e30
f32 = jnp.float32
bf16 = jnp.bfloat16


def rope_tables(positions):
    half = ROPE // 2
    inverse = jnp.exp(-math.log(10000.0) * jnp.arange(half, dtype=f32) * 2.0 / ROPE)
    angles = positions.astype(f32)[:, None] * inverse[None, :]
    angles = jnp.concatenate([angles, angles], axis=-1)
    return (jnp.cos(angles), jnp.sin(angles))


def rotate_half(values):
    half = values.shape[-1] // 2
    return jnp.concatenate([-values[..., half:], values[..., :half]], axis=-1)


def rotate(values, cosine, sine):
    return values * cosine + rotate_half(values) * sine


def unrotate(grads, cosine, sine):
    return grads * cosine - rotate_half(grads) * sine


def rms_inverse(values):
    return lax.rsqrt(jnp.mean(values * values, axis=-1, keepdims=True) + eps)


def norm_backward(grad_out, normed, inverse_rms, gain):
    scaled = grad_out * gain
    return inverse_rms * (scaled - normed * jnp.mean(scaled * normed, axis=-1, keepdims=True))


def dot(left, right, dims):
    return lax.dot_general(left, right, (dims, ((), ())), preferred_element_type=f32)


def round_low(values):
    return lax.reduce_precision(values, 8, 7)


def tp_xor(values, mask):
    size = lax.axis_size("tp")
    return lax.ppermute(values, "tp", [(i, i ^ mask) for i in range(size)])


def from_ctx(values, shift):
    size = lax.axis_size("ctx")
    return lax.ppermute(values, "ctx", [((i + shift) % size, i) for i in range(size)])


def exchange_ctx(parts):
    size = lax.axis_size("ctx")
    me = lax.axis_index("ctx")
    came = [lax.dynamic_index_in_dim(parts, me, 0, False)]
    for shift in range(1, size):
        send = lax.dynamic_index_in_dim(parts, lax.rem(me + shift, size), 0, False)
        came.append(lax.ppermute(send, "ctx", [(i, (i + shift) % size) for i in range(size)]))
    return came


def placed(pieces, places):
    whole = jnp.zeros((len(pieces),) + pieces[0].shape, pieces[0].dtype)
    for piece, place in zip(pieces, places):
        whole = lax.dynamic_update_index_in_dim(whole, piece, place, 0)
    return whole


def gather_ctx(values):
    size = lax.axis_size("ctx")
    me = lax.axis_index("ctx")
    pieces = [values] + [from_ctx(values, shift) for shift in range(1, size)]
    return placed(pieces, [lax.rem(me + shift, size) for shift in range(size)])


def exchange_tp(parts):
    rank = lax.axis_index("tp")
    size = lax.axis_size("tp")
    pieces = [lax.dynamic_index_in_dim(parts, rank, 0, False)]
    for mask in range(1, size):
        pieces.append(tp_xor(lax.dynamic_index_in_dim(parts, rank ^ mask, 0, False), mask))
    return placed(pieces, [rank ^ mask for mask in range(size)])


def pair_order(own, other, second, axis):
    return jnp.concatenate(
        [jnp.where(second, other, own), jnp.where(second, own, other)], axis=axis
    )


def gather_shard(values, axis):
    if lax.axis_size("shard") == 2:
        other = lax.ppermute(values, "shard", [(0, 1), (1, 0)])
        return pair_order(values, other, lax.axis_index("shard") == 1, axis)
    return lax.all_gather(values, "shard", axis=axis, tiled=True)


def scatter_shard(values, axis):
    size = lax.axis_size("shard")
    if size == 2:
        length = values.shape[axis] // 2
        low = lax.slice_in_dim(values, 0, length, axis=axis)
        high = lax.slice_in_dim(values, length, 2 * length, axis=axis)
        second = lax.axis_index("shard") == 1
        keep = jnp.where(second, high, low)
        send = jnp.where(second, low, high).astype(bf16)
        return keep + lax.ppermute(send, "shard", [(0, 1), (1, 0)]).astype(f32)
    return lax.psum_scatter(
        values.astype(bf16), "shard", scatter_dimension=axis, tiled=True
    ).astype(f32)


def scatter_ctx(values):
    me = lax.axis_index("ctx")
    own = lax.dynamic_index_in_dim(values, me, 0, False).astype(f32)
    return sum((piece.astype(f32) for piece in exchange_ctx(values.astype(bf16))[1:]), own)


def gather_tp(chunk):
    rank = lax.axis_index("tp")
    low_bit, high_bit = (rank & 1) == 1, (rank >> 1) == 1
    other = tp_xor(chunk, 2)
    pair = jnp.stack([jnp.where(high_bit, other, chunk), jnp.where(high_bit, chunk, other)])
    across = tp_xor(pair, 1)
    both = jnp.stack(
        [jnp.where(low_bit, across, pair), jnp.where(low_bit, pair, across)], axis=1
    )
    return both.reshape((4,) + chunk.shape)


def scatter_tp(partial_sum):
    rank = lax.axis_index("tp")
    low_bit, high_bit = (rank & 1) == 1, (rank >> 1) == 1
    parts = partial_sum.reshape((2, 2) + partial_sum.shape[1:])
    keep = jnp.where(low_bit, parts[:, 1], parts[:, 0])
    send = jnp.where(low_bit, parts[:, 0], parts[:, 1]).astype(bf16)
    summed = keep + tp_xor(send, 1).astype(f32)
    keep = jnp.where(high_bit, summed[1], summed[0])
    send = jnp.where(high_bit, summed[0], summed[1]).astype(bf16)
    return keep + tp_xor(send, 2).astype(f32)


def after(values, earlier):
    return lax.optimization_barrier((values, earlier))[0]


def shifts():
    size = lax.axis_size("ctx")
    return sorted(range(size), key=lambda shift: (min(shift, size - shift), shift))


def gather_tokens(chunk):
    groups, last = [], None
    for shift in shifts():
        if len(groups) == 3:
            chunk = after(chunk, last)
        here = from_ctx(chunk, shift) if shift else chunk
        if shift and last is None:
            last = here
        far = tp_xor(here, 2)
        near, near_far = tp_xor(here, 1), tp_xor(far, 1)
        groups.append(jnp.concatenate([here, far, near, near_far], axis=0))
    return groups


def scatter_tp_groups(groups):
    result = []
    for group in groups:
        half = group.shape[0] // 2
        summed = group[:half].astype(f32) + tp_xor(group[half:], 1).astype(f32)
        far = tp_xor(summed[half // 2 :].astype(bf16), 2).astype(f32)
        result.append(summed[: half // 2] + far)
    return result


def scatter_ctx_groups(groups, earlier=None):
    size = lax.axis_size("ctx")
    came = [groups[0]]
    for shift, group in list(zip(shifts(), groups))[1:]:
        came.append(
            lax.ppermute(
                group.astype(bf16), "ctx", [(i, (i + shift) % size) for i in range(size)]
            )
        )
    if earlier is not None:
        came = after(came, earlier)
    return sum((piece.astype(f32) for piece in came[1:]), came[0])


def contract(left,right,ld,rd):
    return lax.dot_general(left,right,(((ld,),(rd,)),((),())),preferred_element_type=f32)

def turned(values, keep, ahead, behind):
    return values*keep + pltpu.roll(values, LANES-ROPE//2, 1)*ahead + pltpu.roll(values, ROPE//2, 1)*behind

def padded_query(q_ref, table_ref, head):
    raw = q_ref[0, :, head*HEAD:(head+1)*HEAD]
    raw = jnp.concatenate([raw, jnp.zeros((raw.shape[0], LANES-HEAD), f32)], axis=1)
    return turned(raw, table_ref[0], table_ref[1], table_ref[2]).astype(bf16)

def forward_kernel(heads, q_ref, kv_ref, rotary_ref, table_ref, limit_ref, o_ref, lse_ref, bias_ref):
    rows, keys = bias_ref.shape
    place = lax.broadcasted_iota(jnp.int32, (rows, keys), 1)
    inside = (place >= limit_ref[0, :, 0:1]) & (place <= limit_ref[0, :, 1:2])
    bias_ref[...] = jnp.where(inside, 0.0, big_negative)
    lane = lax.broadcasted_iota(jnp.int32, (rows, LANES), 1)
    key_lane = lax.broadcasted_iota(jnp.int32, (keys, LANES), 1)
    logs = jnp.zeros((rows, LANES), f32)
    held = None
    for head in range(heads):
        query = padded_query(q_ref, table_ref, head)
        kv = kv_ref[0, :, head*LANES:(head+1)*LANES]
        key = jnp.where(key_lane < NOPE, kv, rotary_ref[0])
        scores = contract(query, key, 1, 1)*(score_scale*log2e) + bias_ref[...]
        top = jnp.max(scores, axis=1, keepdims=True)
        weights = jnp.exp2(scores - top)
        total = jnp.sum(weights, axis=1, keepdims=True)
        out = contract(weights.astype(bf16), kv, 1, 0)*(1.0/total)
        logs = jnp.where(lane == head, top + jnp.log2(total), logs)
        if head % 2 == 0:
            held = pltpu.roll(out, VDIM, 1)
        else:
            start = (head//2)*LANES
            o_ref[0, :, start:start+LANES] = jnp.where(lane < VDIM, held, out).astype(bf16)
    lse_ref[0] = logs

def attention_forward(query, kv, rotary, table, limits, heads):
    seqs, rows, _ = query.shape
    keys = kv.shape[1]
    whole = lambda *dims: pl.BlockSpec((1,)+dims, lambda s: (s,)+(0,)*len(dims))
    return pl.pallas_call(
        functools.partial(forward_kernel, heads),
        grid=(seqs,),
        in_specs=[whole(*query.shape[1:]), whole(*kv.shape[1:]), whole(*rotary.shape[1:]),
                  pl.BlockSpec(table.shape, lambda s:(0,0,0)), whole(*limits.shape[1:])],
        out_specs=[whole(rows, heads*VDIM), whole(rows, LANES)],
        out_shape=[jax.ShapeDtypeStruct((seqs,rows,heads*VDIM),bf16), jax.ShapeDtypeStruct((seqs,rows,LANES),f32)],
        scratch_shapes=[pltpu.VMEM((rows,keys),f32)],
        compiler_params=pltpu.CompilerParams(vmem_limit_bytes=50*1024*1024),
        cost_estimate=pl.CostEstimate(flops=seqs*heads*rows*keys*4*LANES, bytes_accessed=12_000_000, transcendentals=seqs*heads*rows*keys),
    )(query, kv, rotary, table, limits)

def backward_kernel(heads, q_ref, kv_ref, rotary_ref, table_ref, limit_ref, lse_ref, go_ref, gq_ref, gkv_ref, gkr_ref, bias_ref):
    keys, rows = bias_ref.shape
    place = lax.broadcasted_iota(jnp.int32, (keys, rows), 0)
    inside = (place >= limit_ref[0, 0:1, :]) & (place <= limit_ref[0, 1:2, :])
    bias_ref[...] = jnp.where(inside, 0.0, big_negative)
    lane = lax.broadcasted_iota(jnp.int32, (rows, LANES), 1)
    key_lane = lax.broadcasted_iota(jnp.int32, (keys, LANES), 1)
    logs = lse_ref[0].T
    grad_rotary = jnp.zeros((keys, LANES), f32)
    for head in range(heads):
        query = padded_query(q_ref, table_ref, head)
        kv = kv_ref[0, :, head*LANES:(head+1)*LANES]
        key = jnp.where(key_lane < NOPE, kv, rotary_ref[0])
        start = (head//2)*LANES
        go = go_ref[0, :, start:start+LANES].astype(f32)
        if head % 2 == 0:
            go = pltpu.roll(go, VDIM, 1)
        go = jnp.where(lane < VDIM, 0.0, go).astype(bf16)
        scores = contract(key, query, 1, 1)*(score_scale*log2e) + bias_ref[...]
        prob = jnp.exp2(scores - logs[head:head+1, :])
        grad_prob = contract(kv, go, 1, 1)
        grad_value = contract(prob.astype(bf16), go, 1, 0)
        mixed = jnp.sum(prob*grad_prob, axis=0, keepdims=True)
        grad_scores = (prob*(grad_prob - mixed)).astype(bf16)
        grad_key = contract(grad_scores, query, 1, 0)*score_scale
        grad_rotary = grad_rotary + grad_key
        gkv_ref[0, :, head*LANES:(head+1)*LANES] = jnp.where(key_lane < NOPE, grad_key, grad_value).astype(bf16)
        grad_query = contract(key, grad_scores, 0, 0).T*score_scale
        grad_query = turned(grad_query, table_ref[0], -table_ref[1], -table_ref[2])
        gq_ref[0, :, head*HEAD:(head+1)*HEAD] = grad_query[:, :HEAD].astype(bf16)
    gkr_ref[0] = grad_rotary

def attention_backward(query, kv, rotary, table, limits, lse, go, heads):
    seqs, rows, _ = query.shape
    keys = kv.shape[1]
    whole = lambda *dims: pl.BlockSpec((1,)+dims, lambda s: (s,)+(0,)*len(dims))
    return pl.pallas_call(
        functools.partial(backward_kernel, heads),
        grid=(seqs,),
        in_specs=[whole(*query.shape[1:]), whole(*kv.shape[1:]), whole(*rotary.shape[1:]),
                  pl.BlockSpec(table.shape, lambda s:(0,0,0)), whole(*limits.shape[1:]), whole(*lse.shape[1:]), whole(*go.shape[1:])],
        out_specs=[whole(rows, heads*HEAD), whole(keys, heads*LANES), whole(keys, LANES)],
        out_shape=[jax.ShapeDtypeStruct((seqs,rows,heads*HEAD),bf16), jax.ShapeDtypeStruct((seqs,keys,heads*LANES),bf16), jax.ShapeDtypeStruct((seqs,keys,LANES),f32)],
        scratch_shapes=[pltpu.VMEM((keys,rows),f32)],
        compiler_params=pltpu.CompilerParams(vmem_limit_bytes=58*1024*1024),
        cost_estimate=pl.CostEstimate(flops=seqs*heads*rows*keys*10*LANES, bytes_accessed=20_000_000, transcendentals=seqs*heads*rows*keys),
    )(query, kv, rotary, table, limits, lse, go)


def halves(count, length):
    if count == 1:
        return [0]
    second = lax.axis_index("shard")
    return [pl.multiple_of(second * length, LANES), pl.multiple_of((1 - second) * length, LANES)]


def weights_kernel(n_group, n_piece, *refs):
    refs = list(refs)

    def take(count):
        return [refs.pop(0) for _ in range(count)]

    tokens = [take(n_piece) for _ in range(n_group)]
    grads = [take(n_piece) for _ in range(n_group)]
    kept = [take(3) for _ in range(n_group)]
    down_out, gate_out, up_out = refs
    down = gate = up = 0.0
    for group in range(n_group):
        token = jnp.concatenate([piece[...] for piece in tokens[group]], axis=0)
        grad = jnp.concatenate([piece[...] for piece in grads[group]], axis=0)
        hidden, grad_gate, grad_up = kept[group]
        down = down + contract(hidden[...], grad, 1, 0)
        gate = gate + contract(grad_gate[...], token, 1, 0)
        up = up + contract(grad_up[...], token, 1, 0)
    down_out[...] = down.astype(bf16)
    gate_out[...] = gate.astype(bf16)
    up_out[...] = up.astype(bf16)


def ffn_weight_grads(tokens, grads, kept):
    n_group, n_piece = len(tokens), len(tokens[0])
    rows, width = tokens[0][0].shape
    units = kept[0][0].shape[0]
    step = 512

    def column(height):
        return pl.BlockSpec((height, step), lambda i: (0, i))

    whole = pl.BlockSpec(kept[0][0].shape, lambda i: (0, 0))
    flat = [piece for group in tokens for piece in group]
    flat += [piece for group in grads for piece in group]
    total = rows * n_piece * n_group
    return pl.pallas_call(
        functools.partial(weights_kernel, n_group, n_piece),
        grid=(width // step,),
        in_specs=[column(rows)] * len(flat) + [whole] * (3 * n_group),
        out_specs=[column(units)] * 3,
        out_shape=[jax.ShapeDtypeStruct((units, width), bf16)] * 3,
        compiler_params=pltpu.CompilerParams(vmem_limit_bytes=48 * MIB),
        cost_estimate=pl.CostEstimate(
            flops=6 * total * width * units, bytes_accessed=33_000_000, transcendentals=0
        ),
    )(*flat, *[array for group in kept for array in group])


def by_ctx(size, write):
    me = lax.axis_index("ctx")
    for place in range(size):

        @pl.when(me == place)
        def _(place=place):
            write(place)


def join_kernel(size, *refs):
    length = refs[0].shape[1]
    out_ref = refs[-1]

    def write(me):
        for k in range(size):
            block = (me - k) % size
            out_ref[:, block * length : (block + 1) * length] = refs[k][...]

    by_ctx(size, write)


def join_columns(pieces):
    size = len(pieces)
    height, length = pieces[0].shape
    return pl.pallas_call(
        functools.partial(join_kernel, size),
        out_shape=jax.ShapeDtypeStruct((height, size * length), pieces[0].dtype),
        compiler_params=pltpu.CompilerParams(vmem_limit_bytes=16 * MIB),
        cost_estimate=pl.CostEstimate(
            flops=0, bytes_accessed=4 * size * pieces[0].size, transcendentals=0
        ),
    )(*pieces)


def place_kernel(size, turn, *refs):
    out_ref = refs[-1]
    height = refs[0].shape[0]

    def write(me):
        for k in range(size):
            block = (me - k) % size
            piece = refs[k][...].astype(f32)
            if turn:
                out_ref[:, block * height : (block + 1) * height] = piece.T
            else:
                out_ref[block * height : (block + 1) * height, :] = piece

    by_ctx(size, write)


def place_rows(pieces, turn):
    size = len(pieces)
    height, length = pieces[0].shape
    shape = (length, size * height) if turn else (size * height, length)
    return pl.pallas_call(
        functools.partial(place_kernel, size, turn),
        out_shape=jax.ShapeDtypeStruct(shape, f32),
        compiler_params=pltpu.CompilerParams(vmem_limit_bytes=24 * MIB),
        cost_estimate=pl.CostEstimate(
            flops=0, bytes_accessed=6 * size * pieces[0].size, transcendentals=0
        ),
    )(*pieces)


def split_kernel(n_half, keep_ref, came_ref, out_ref):
    n, height, length = out_ref.shape
    keep = keep_ref[:, pl.ds(halves(n_half, n * length)[0], n * length)].astype(f32)
    total = (keep + came_ref[...].astype(f32)).astype(bf16)
    for i in range(n):
        out_ref[i] = total[:, i * length : (i + 1) * length]


def add_and_split(values, came, n):
    height, length = came.shape
    return pl.pallas_call(
        functools.partial(split_kernel, values.shape[1] // length),
        out_shape=jax.ShapeDtypeStruct((n, height, length // n), bf16),
        compiler_params=pltpu.CompilerParams(vmem_limit_bytes=24 * MIB),
        cost_estimate=pl.CostEstimate(flops=0, bytes_accessed=6 * came.size, transcendentals=0),
    )(values, came)


def on_device(
    hidden_in,
    cotangent,
    doc_lengths,
    attn_gain,
    q_gain,
    kv_gain,
    ffn_gain,
    q_down,
    kv_down,
    q_up,
    kv_up,
    out_proj,
    gate_proj,
    up_proj,
    down_proj,
):
    seqs, piece, width = hidden_in.shape
    n_shard, n_ctx, n_tp = lax.axis_size("shard"), lax.axis_size("ctx"), lax.axis_size("tp")
    rank = lax.axis_index("tp")
    low_bit = (rank & 1) == 1
    rows = seqs * piece
    chunk_rows = rows // n_tp
    seq_len = piece * n_ctx
    offset = lax.axis_index("ctx") * piece
    q_part, kv_part = QRANK // n_tp, (KVRANK + ROPE) // n_tp
    part = q_part + kv_part
    block = q_down.shape[0]
    n_gain = 2 * attn_gain.shape[0] + q_gain.shape[0] + kv_gain.shape[0]

    gain_row = jnp.concatenate([attn_gain, ffn_gain, q_gain, kv_gain])
    n_blocks = n_shard * n_ctx * n_tp
    everywhere = ("shard", "ctx", "tp")
    gains = lax.all_to_all(
        jnp.broadcast_to(gain_row[None, None], (n_blocks, 1, n_gain)), everywhere, 0, 0
    )
    gains = gains[:, 0].astype(f32)
    cut = attn_gain.shape[0]
    gain_attn = gains[:, :cut].reshape(1, -1)
    gain_ffn = gains[:, cut : 2 * cut].reshape(1, -1)
    gain_query = gains[:, 2 * cut : 2 * cut + q_gain.shape[0]].reshape(1, -1)
    gain_latent = gains[:, 2 * cut + q_gain.shape[0] :].reshape(1, -1)

    small = jnp.stack(
        [
            jnp.concatenate(
                [
                    q_down[:, i * q_part : (i + 1) * q_part],
                    kv_down[:, i * kv_part : (i + 1) * kv_part],
                ],
                axis=1,
            )
            for i in range(n_tp)
        ]
    )
    small = gather_ctx(exchange_tp(small).reshape(-1, part))
    q_up, kv_up, out_proj, gate_proj, up_proj, down_proj = lax.optimization_barrier(
        (q_up, kv_up, out_proj, gate_proj, up_proj, down_proj, small)
    )[:6]
    down_part = gather_shard(small.reshape(-1, part), 0)

    up_query = gather_ctx(q_up)
    up_latent = gather_ctx(kv_up)
    up_query = gather_shard(up_query.reshape(-1, q_up.shape[1]), 0)
    up_latent = gather_shard(up_latent.reshape(-1, kv_up.shape[1]), 0)
    out_full = lax.all_gather(out_proj, ("shard", "ctx"), axis=1, tiled=True)

    heads = up_query.shape[1] // HEAD
    positions = offset + jnp.arange(piece, dtype=jnp.int32)
    cosine_here, sine_here = rope_tables(positions)
    docs = doc_lengths.shape[1]
    ends = jnp.stack([jnp.sum(doc_lengths[:, : i + 1], axis=1) for i in range(docs)], axis=1)
    starts = jnp.max(
        jnp.where(positions[None, :, None] >= ends[:, None, :], ends[:, None, :], 0), axis=-1
    )
    limits = jnp.stack([starts, jnp.broadcast_to(positions[None], starts.shape)], axis=1)
    cosine, sine = cosine_here[:, : ROPE // 2], sine_here[:, : ROPE // 2]
    zero, fill = jnp.zeros_like(cosine), jnp.zeros((piece, LANES - HEAD), f32)
    plain = jnp.zeros((piece, NOPE), f32)
    table = jnp.stack(
        [
            jnp.concatenate([plain + 1.0, cosine, cosine, fill], axis=1),
            jnp.concatenate([plain, -sine, zero, fill], axis=1),
            jnp.concatenate([plain, zero, sine, fill], axis=1),
        ]
    )

    stream = hidden_in.astype(f32).reshape(rows, width)
    grad_out = cotangent.astype(f32).reshape(rows, width)
    chunk_start = rank * chunk_rows

    def own_chunk(values):
        return lax.dynamic_slice_in_dim(values, chunk_start, chunk_rows, 0)

    inverse_one = rms_inverse(stream)
    normed_one = stream * inverse_one
    input_low = (normed_one * gain_attn).astype(bf16)
    low_rank = gather_tp(dot(input_low, down_part, ((1,), (0,))))
    query_latent = low_rank[:, :, :q_part].transpose(1, 0, 2).reshape(rows, QRANK)
    latent_raw = low_rank[:, :, q_part:].transpose(1, 0, 2).reshape(rows, KVRANK + ROPE)
    inverse_latent = rms_inverse(latent_raw[:, :KVRANK])
    normed_latent = latent_raw[:, :KVRANK] * inverse_latent
    latent_low = (normed_latent * gain_latent).astype(bf16).reshape(seqs, piece, KVRANK)
    rotary_key = rotate(
        latent_raw[:, KVRANK:].reshape(seqs, piece, ROPE), cosine_here, sine_here
    ).astype(bf16)
    keys_here = jnp.concatenate(
        [latent_low, jnp.pad(rotary_key, ((0, 0), (0, 0), (NOPE, LANES - HEAD)))], axis=-1
    )
    half = seqs // 2
    mine = rank & 1
    keys_mine = lax.dynamic_slice_in_dim(keys_here, mine * half, half, 0)
    keys_mine = gather_ctx(keys_mine)
    keys_mine = keys_mine.transpose(1, 0, 2, 3).reshape(half, seq_len, KVRANK + LANES)
    keys_all = pair_order(keys_mine, tp_xor(keys_mine, 1), low_bit, 0)
    latent_all, rotary_all = keys_all[..., :KVRANK], keys_all[..., KVRANK:]

    grad_ffn = lax.all_gather(
        after((res_scale * own_chunk(grad_out)).astype(bf16), low_rank), ("ctx", "tp"), axis=0
    )
    grad_ffn_groups = []
    for shift in shifts():
        place = lax.rem(lax.axis_index("ctx") + shift, n_ctx) * n_tp
        grad_ffn_groups.append(
            jnp.concatenate(
                [
                    lax.dynamic_index_in_dim(grad_ffn, place + (rank ^ i), 0, False)
                    for i in (0, 2, 1, 3)
                ],
                axis=0,
            )
        )

    def hidden_rows(weight):
        return exchange_ctx(weight.reshape(n_ctx, -1, weight.shape[1]))

    gate_pieces, up_pieces = hidden_rows(gate_proj.T), hidden_rows(up_proj.T)
    down_pieces = hidden_rows(down_proj)

    down_all = gather_tp(after(down_part, keys_all))
    down_query = down_all[:, :, :q_part].transpose(1, 0, 2).reshape(width, QRANK)
    down_latent = down_all[:, :, q_part:].transpose(1, 0, 2).reshape(width, KVRANK + ROPE)

    inverse_query = rms_inverse(query_latent)
    normed_query = query_latent * inverse_query
    query_low = (normed_query * gain_query).astype(bf16)
    key_value = jnp.einsum("slr,rf->slf", latent_all, up_latent, preferred_element_type=f32)
    key_value = key_value.astype(bf16)
    query = dot(query_low, up_query, ((1,), (0,))).reshape(seqs, piece, -1)
    attended_low, log_total = attention_forward(
        query, key_value, rotary_all, table, limits.transpose(0, 2, 1), heads
    )
    attended_low = attended_low.reshape(rows, heads * VDIM)
    gate_full = gather_shard(join_columns(after(gate_pieces, attended_low)), 1)

    attn_out = scatter_tp(
        dot(attended_low, out_full, ((1,), (0,))).reshape(n_tp, chunk_rows, width)
    )
    upward_full = gather_shard(join_columns(after(up_pieces, attn_out)), 1)
    down_full = gather_shard(join_columns(after(down_pieces, attn_out)), 1)
    middle = own_chunk(stream) + res_scale * attn_out
    inverse_two = rms_inverse(middle)
    normed_two = middle * inverse_two
    ffn_groups = gather_tokens((normed_two * gain_ffn).astype(bf16))

    ffn_parts, grad_two_parts, kept = [], [], []
    for ffn_low, grad_low in zip(ffn_groups, grad_ffn_groups):
        gate_value = dot(ffn_low, gate_full, ((1,), (1,)))
        up_value = dot(ffn_low, upward_full, ((1,), (1,)))
        sigma = jax.nn.sigmoid(gate_value)
        gate_act = gate_value * sigma
        hidden_low = (gate_act * up_value).astype(bf16)
        grad_hidden = dot(grad_low, down_full, ((1,), (1,)))
        grad_gate = (grad_hidden * up_value * sigma * (1.0 + gate_value * (1.0 - sigma))).astype(
            bf16
        )
        grad_upward = (grad_hidden * gate_act).astype(bf16)
        grad_two_part = dot(grad_gate, gate_full, ((1,), (0,)))
        grad_two_part = grad_two_part + dot(grad_upward, upward_full, ((1,), (0,)))
        grad_two_parts.append(grad_two_part.astype(bf16))
        ffn_parts.append(dot(hidden_low, down_full, ((1,), (0,))).astype(bf16))
        kept.append((hidden_low.T, grad_gate.T, grad_upward.T))

    grad_two_parts = scatter_tp_groups(grad_two_parts)
    grad_down_w, grad_gate_w, grad_upward_w = ffn_weight_grads(
        [[group] for group in ffn_groups], [[group] for group in grad_ffn_groups], kept
    )
    grad_two = scatter_ctx_groups(grad_two_parts, grad_gate_w)
    ffn_parts = scatter_tp_groups(after(ffn_parts, grad_two_parts))
    grad_middle = own_chunk(grad_out) + norm_backward(grad_two, normed_two, inverse_two, gain_ffn)
    grad_gain_ffn = jnp.sum(grad_two * normed_two, axis=0)
    grad_attn = gather_tp((res_scale * grad_middle).astype(bf16)).reshape(rows, width)

    grad_out_w = lax.psum_scatter(
        dot(attended_low, grad_attn, ((0,), (0,))).astype(bf16),
        ("shard", "ctx"),
        scatter_dimension=1,
        tiled=True,
    ).astype(f32)

    grad_attended = dot(grad_attn, out_full, ((1,), (1,))).astype(bf16)
    grad_query, grad_key_value, grad_krope = attention_backward(
        query,
        key_value,
        rotary_all,
        table,
        limits,
        log_total,
        grad_attended.reshape(seqs, piece, -1),
        heads,
    )
    grad_query = grad_query.reshape(rows, heads * HEAD)
    grad_key_value = grad_key_value.reshape(seqs * seq_len, heads * (NOPE + VDIM))

    grad_keys = dot(grad_key_value, up_latent, ((1,), (1,))).astype(bf16)
    grad_keys = jnp.concatenate(
        [grad_keys.reshape(seqs, seq_len, KVRANK), grad_krope.astype(bf16)], axis=-1
    )

    def add_near(values):
        keep = lax.dynamic_slice_in_dim(values, mine * half, half, 0)
        send = lax.dynamic_slice_in_dim(values, (1 - mine) * half, half, 0)
        return keep.astype(f32) + tp_xor(send, 1).astype(f32)

    grad_keys = add_near(grad_keys).astype(bf16)
    grad_keys = scatter_ctx(
        grad_keys.reshape(half, n_ctx, piece, KVRANK + LANES).transpose(1, 0, 2, 3)
    )
    grad_pre_query = dot(grad_query, up_query, ((1,), (1,))).astype(bf16)
    grad_pre_query = add_near(grad_pre_query.reshape(seqs, piece, QRANK))
    grad_low = jnp.concatenate([grad_pre_query, grad_keys], axis=-1).astype(bf16)
    grad_low = (grad_low.astype(f32) + tp_xor(grad_low, 2).astype(f32)).astype(bf16)
    grad_low = pair_order(grad_low, tp_xor(grad_low, 1), low_bit, 0)
    grad_low = grad_low.reshape(rows, QRANK + KVRANK + LANES).astype(f32)

    grad_out_query, grad_out_latent = grad_low[:, :QRANK], grad_low[:, QRANK : QRANK + KVRANK]
    grad_query_latent = norm_backward(grad_out_query, normed_query, inverse_query, gain_query)
    grad_compressed = norm_backward(grad_out_latent, normed_latent, inverse_latent, gain_latent)
    grad_gain_query = jnp.sum(own_chunk(grad_out_query * normed_query), axis=0)
    grad_gain_latent = jnp.sum(own_chunk(grad_out_latent * normed_latent), axis=0)
    grad_rotary = grad_low[:, QRANK + KVRANK + NOPE : QRANK + KVRANK + HEAD]
    grad_rotary = grad_rotary.reshape(seqs, piece, ROPE)
    grad_rotary = unrotate(grad_rotary, cosine_here, sine_here).reshape(rows, ROPE)
    grad_query_latent = grad_query_latent.astype(bf16)
    grad_latent_raw = jnp.concatenate([grad_compressed, grad_rotary], axis=-1).astype(bf16)

    grad_pre_one = dot(own_chunk(grad_query_latent), down_query, ((1,), (1,)))
    grad_pre_one = grad_pre_one + dot(own_chunk(grad_latent_raw), down_latent, ((1,), (1,)))
    normed_own = own_chunk(normed_one)
    grad_input = grad_middle + norm_backward(
        grad_pre_one, normed_own, own_chunk(inverse_one), gain_attn
    )
    grad_gain_attn = jnp.sum(grad_pre_one * normed_own, axis=0)
    grad_input = gather_tp(round_low(grad_input).astype(bf16)).astype(f32)

    grad_part = jnp.concatenate(
        [
            lax.dynamic_slice_in_dim(grad_query_latent, rank * q_part, q_part, 1),
            lax.dynamic_slice_in_dim(grad_latent_raw, rank * kv_part, kv_part, 1),
        ],
        axis=1,
    )
    grad_small = dot(input_low, grad_part, ((0,), (0,)))
    grad_small = scatter_ctx(
        scatter_shard(grad_small, 0).reshape(n_ctx, n_tp, block, part)
    )
    grad_small = exchange_tp(grad_small.astype(bf16)).astype(f32).transpose(1, 0, 2)
    grad_down_query = grad_small[:, :, :q_part].reshape(block, QRANK)
    grad_down_latent = grad_small[:, :, q_part:].reshape(block, KVRANK + ROPE)
    grad_gains = jnp.concatenate(
        [
            grad_gain_attn.reshape(n_blocks, -1),
            grad_gain_ffn.reshape(n_blocks, -1),
            grad_gain_query.reshape(n_blocks, -1),
            grad_gain_latent.reshape(n_blocks, -1),
        ],
        axis=1,
    )
    grad_gains = lax.all_to_all(grad_gains[:, None], everywhere, 0, 0)
    grad_gains = jnp.sum(grad_gains[:, 0], axis=0)

    grad_down_w, grad_query, grad_key_value = lax.optimization_barrier(
        (grad_down_w, grad_query, grad_key_value, grad_keys)
    )[:3]
    output = round_low(middle + res_scale * scatter_ctx_groups(ffn_parts, grad_keys))
    output = gather_tp(output.astype(bf16)).astype(f32)

    def rows_grad(grad):
        mine = scatter_shard(grad, 0)
        return scatter_ctx(mine.reshape(n_ctx, -1, mine.shape[-1]))

    grad_up_query = rows_grad(dot(query_low, grad_query, ((0,), (0,))))
    grad_up_latent = rows_grad(
        dot(latent_all.reshape(-1, KVRANK), grad_key_value, ((0,), (0,)))
    )
    def hidden_grad(grad):
        length = grad.shape[1] // n_shard
        if n_shard == 2:
            other = 1 - lax.axis_index("shard")
            send = lax.dynamic_slice_in_dim(grad, other * length, length, 1)
            came = lax.ppermute(send, "shard", [(0, 1), (1, 0)])
            parts = add_and_split(grad, came, n_ctx)
        else:
            mine = scatter_shard(grad, 1).astype(bf16)
            parts = mine.reshape(mine.shape[0], n_ctx, -1).transpose(1, 0, 2)
        return parts

    grad_gate_w = exchange_ctx(hidden_grad(after(grad_gate_w, grad_attn)))
    grad_upward_w = exchange_ctx(hidden_grad(after(grad_upward_w, grad_attn)))
    grad_gate_w = place_rows(after(grad_gate_w, grad_low), True)
    grad_upward_w = place_rows(after(grad_upward_w, grad_low), True)
    grad_down_w = place_rows(exchange_ctx(hidden_grad(grad_down_w)), False)
    return (
        output.reshape(seqs, piece, width),
        grad_input.reshape(seqs, piece, width),
        grad_gains[:cut],
        grad_gains[2 * cut : 2 * cut + q_gain.shape[0]],
        grad_gains[2 * cut + q_gain.shape[0] :],
        grad_gains[cut : 2 * cut],
        grad_down_query,
        grad_down_latent,
        grad_up_query,
        grad_up_latent,
        grad_out_w,
        grad_gate_w,
        grad_upward_w,
        grad_down_w,
    )


def solution(mesh):
    all_axes = ("shard", "ctx", "tp")
    tokens, vector, square = P("shard", "ctx", None), P(all_axes), P(all_axes, None)
    inner, outer = P(("shard", "ctx"), "tp"), P("tp", ("shard", "ctx"))
    weights = (
        vector,
        vector,
        vector,
        vector,
        square,
        square,
        inner,
        inner,
        outer,
        inner,
        inner,
        outer,
    )
    return jax.shard_map(
        on_device,
        mesh=mesh,
        in_specs=(tokens, tokens, P("shard", None)) + weights,
        out_specs=(tokens, tokens) + weights,
        check_vma=False,
    )
```

```python
import functools
import math

import jax
import jax.numpy as jnp
from jax import lax
from jax.experimental import pallas as pl
from jax.experimental.pallas import tpu as pltpu
from jax.sharding import PartitionSpec as P

NOPE = 64
ROPE = 32
VDIM = 64
KVRANK = 256
QRANK = 768
LANES = 128
HEAD = NOPE + ROPE
score_scale = 1.0 / math.sqrt(HEAD)
log2e = 1.0 / math.log(2.0)
MIB = 1024 * 1024

eps = 1e-05
res_scale = 1.4 / math.sqrt(62.0)
big_negative = -1e30
f32 = jnp.float32
bf16 = jnp.bfloat16


def rope_tables(positions):
    half = ROPE // 2
    inverse = jnp.exp(-math.log(10000.0) * jnp.arange(half, dtype=f32) * 2.0 / ROPE)
    angles = positions.astype(f32)[:, None] * inverse[None, :]
    angles = jnp.concatenate([angles, angles], axis=-1)
    return (jnp.cos(angles), jnp.sin(angles))


def rotate_half(values):
    half = values.shape[-1] // 2
    return jnp.concatenate([-values[..., half:], values[..., :half]], axis=-1)


def rotate(values, cosine, sine):
    return values * cosine + rotate_half(values) * sine


def unrotate(grads, cosine, sine):
    return grads * cosine - rotate_half(grads) * sine


def rms_inverse(values):
    return lax.rsqrt(jnp.mean(values * values, axis=-1, keepdims=True) + eps)


def norm_backward(grad_out, normed, inverse_rms, gain):
    scaled = grad_out * gain
    return inverse_rms * (scaled - normed * jnp.mean(scaled * normed, axis=-1, keepdims=True))


def dot(left, right, dims):
    return lax.dot_general(left, right, (dims, ((), ())), preferred_element_type=f32)


def round_low(values):
    return lax.reduce_precision(values, 8, 7)


def tp_xor(values, mask):
    size = lax.axis_size("tp")
    return lax.ppermute(values, "tp", [(i, i ^ mask) for i in range(size)])


def from_ctx(values, shift):
    size = lax.axis_size("ctx")
    return lax.ppermute(values, "ctx", [((i + shift) % size, i) for i in range(size)])


def exchange_ctx(parts):
    size = lax.axis_size("ctx")
    me = lax.axis_index("ctx")
    came = [lax.dynamic_index_in_dim(parts, me, 0, False)]
    for shift in range(1, size):
        send = lax.dynamic_index_in_dim(parts, lax.rem(me + shift, size), 0, False)
        came.append(lax.ppermute(send, "ctx", [(i, (i + shift) % size) for i in range(size)]))
    return came


def placed(pieces, places):
    whole = jnp.zeros((len(pieces),) + pieces[0].shape, pieces[0].dtype)
    for piece, place in zip(pieces, places):
        whole = lax.dynamic_update_index_in_dim(whole, piece, place, 0)
    return whole


def gather_ctx(values):
    size = lax.axis_size("ctx")
    me = lax.axis_index("ctx")
    pieces = [values] + [from_ctx(values, shift) for shift in range(1, size)]
    return placed(pieces, [lax.rem(me + shift, size) for shift in range(size)])


def exchange_tp(parts):
    rank = lax.axis_index("tp")
    size = lax.axis_size("tp")
    pieces = [lax.dynamic_index_in_dim(parts, rank, 0, False)]
    for mask in range(1, size):
        pieces.append(tp_xor(lax.dynamic_index_in_dim(parts, rank ^ mask, 0, False), mask))
    return placed(pieces, [rank ^ mask for mask in range(size)])


def pair_order(own, other, second, axis):
    return jnp.concatenate(
        [jnp.where(second, other, own), jnp.where(second, own, other)], axis=axis
    )


def gather_shard(values, axis):
    if lax.axis_size("shard") == 2:
        other = lax.ppermute(values, "shard", [(0, 1), (1, 0)])
        return pair_order(values, other, lax.axis_index("shard") == 1, axis)
    return lax.all_gather(values, "shard", axis=axis, tiled=True)


def scatter_shard(values, axis):
    size = lax.axis_size("shard")
    if size == 2:
        length = values.shape[axis] // 2
        low = lax.slice_in_dim(values, 0, length, axis=axis)
        high = lax.slice_in_dim(values, length, 2 * length, axis=axis)
        second = lax.axis_index("shard") == 1
        keep = jnp.where(second, high, low)
        send = jnp.where(second, low, high).astype(bf16)
        return keep + lax.ppermute(send, "shard", [(0, 1), (1, 0)]).astype(f32)
    return lax.psum_scatter(
        values.astype(bf16), "shard", scatter_dimension=axis, tiled=True
    ).astype(f32)


def scatter_ctx(values):
    me = lax.axis_index("ctx")
    own = lax.dynamic_index_in_dim(values, me, 0, False).astype(f32)
    return sum((piece.astype(f32) for piece in exchange_ctx(values.astype(bf16))[1:]), own)


def gather_tp(chunk):
    rank = lax.axis_index("tp")
    low_bit, high_bit = (rank & 1) == 1, (rank >> 1) == 1
    other = tp_xor(chunk, 2)
    pair = jnp.stack([jnp.where(high_bit, other, chunk), jnp.where(high_bit, chunk, other)])
    across = tp_xor(pair, 1)
    both = jnp.stack(
        [jnp.where(low_bit, across, pair), jnp.where(low_bit, pair, across)], axis=1
    )
    return both.reshape((4,) + chunk.shape)


def scatter_tp(partial_sum, *earlier):
    rank = lax.axis_index("tp")
    low_bit, high_bit = (rank & 1) == 1, (rank >> 1) == 1
    parts = partial_sum.reshape((2, 2) + partial_sum.shape[1:])
    keep = jnp.where(low_bit, parts[:, 1], parts[:, 0])
    send = jnp.where(low_bit, parts[:, 0], parts[:, 1]).astype(bf16)
    summed = keep + tp_xor(send, 1).astype(f32)
    keep = jnp.where(high_bit, summed[1], summed[0])
    send = jnp.where(high_bit, summed[0], summed[1]).astype(bf16)
    if earlier:
        send = after(send, *earlier)
    return keep + tp_xor(send, 2).astype(f32)


def after_kernel(*refs):
    pass


def after(values, *earlier):
    anywhere = pl.BlockSpec(memory_space=pl.ANY)
    return pl.pallas_call(
        after_kernel,
        in_specs=[anywhere] * (1 + len(earlier)),
        out_specs=anywhere,
        out_shape=jax.ShapeDtypeStruct(values.shape, values.dtype),
        input_output_aliases={0: 0},
        cost_estimate=pl.CostEstimate(flops=0, bytes_accessed=0, transcendentals=0),
    )(values, *earlier)


def swap(values, axis, mask):
    size = lax.axis_size(axis)
    return lax.ppermute(values, axis, [(i, i ^ mask) for i in range(size)])


WAYS = {"x": ("tp", 2, 0), "y": ("shard", 1, 1), "z": ("ctx", 1, 2)}
ORDERS = (("x", "y", "z"), ("y", "z", "x"), ("z", "x", "y"))


def column_cuts(width):
    tiles = width // LANES
    cuts = [0, (tiles + 2) // 3, (tiles + 2) // 3 + (tiles + 1) // 3, tiles]
    return [cut * LANES for cut in cuts]


def gather_tokens(chunk, *earlier):
    cuts = column_cuts(chunk.shape[1])
    parts = [
        chunk[None, None, None, :, cuts[i] : cuts[i + 1]] for i in range(len(ORDERS))
    ]
    for step in range(3):
        if step == 1 and earlier:
            parts[0] = after(parts[0], *earlier)
        for i, order in enumerate(ORDERS):
            axis, mask, dim = WAYS[order[step]]
            parts[i] = jnp.concatenate([parts[i], swap(parts[i], axis, mask)], axis=dim)
    whole = jnp.concatenate(parts, axis=-1)
    return whole.reshape(-1, chunk.shape[1])


def scatter_near(own, other):
    return (own.astype(f32) + swap(other, "tp", 1).astype(f32)).astype(bf16)


def scatter_step(parts, step):
    result = []
    for part, order in zip(parts, ORDERS):
        axis, mask, dim = WAYS[order[step]]
        keep = lax.slice_in_dim(part, 0, 1, axis=dim)
        send = lax.slice_in_dim(part, 1, 2, axis=dim)
        summed = keep.astype(f32) + swap(send, axis, mask).astype(f32)
        result.append(summed.astype(bf16) if step else summed)
    return result


def scatter_begin(total):
    cuts = column_cuts(total.shape[1])
    total = total.reshape(2, 2, 2, -1, total.shape[1])
    return [total[..., cuts[i] : cuts[i + 1]] for i in range(len(ORDERS))]


def scatter_end(parts):
    whole = jnp.concatenate(parts, axis=-1)
    return whole.reshape(-1, whole.shape[-1])


def scatter_tokens(total):
    parts = scatter_begin(total)
    for step in reversed(range(3)):
        parts = scatter_step(parts, step)
    return scatter_end(parts)


def contract(left,right,ld,rd):
    return lax.dot_general(left,right,(((ld,),(rd,)),((),())),preferred_element_type=f32)

def turned(values, keep, ahead, behind):
    return values*keep + pltpu.roll(values, LANES-ROPE//2, 1)*ahead + pltpu.roll(values, ROPE//2, 1)*behind

def padded_query(q_ref, table_ref, head):
    raw = q_ref[0, :, head*HEAD:(head+1)*HEAD]
    raw = jnp.concatenate([raw, jnp.zeros((raw.shape[0], LANES-HEAD), f32)], axis=1)
    return turned(raw, table_ref[0], table_ref[1], table_ref[2]).astype(bf16)

def forward_kernel(heads, q_ref, kv_ref, rotary_ref, table_ref, limit_ref, o_ref, lse_ref, bias_ref):
    rows, keys = bias_ref.shape
    place = lax.broadcasted_iota(jnp.int32, (rows, keys), 1)
    inside = (place >= limit_ref[0, :, 0:1]) & (place <= limit_ref[0, :, 1:2])
    bias_ref[...] = jnp.where(inside, 0.0, big_negative)
    lane = lax.broadcasted_iota(jnp.int32, (rows, LANES), 1)
    key_lane = lax.broadcasted_iota(jnp.int32, (keys, LANES), 1)
    logs = jnp.zeros((rows, LANES), f32)
    held = None
    for head in range(heads):
        query = padded_query(q_ref, table_ref, head)
        kv = kv_ref[0, :, head*LANES:(head+1)*LANES]
        key = jnp.where(key_lane < NOPE, kv, rotary_ref[0])
        scores = contract(query, key, 1, 1)*(score_scale*log2e) + bias_ref[...]
        top = jnp.max(scores, axis=1, keepdims=True)
        weights = jnp.exp2(scores - top)
        total = jnp.sum(weights, axis=1, keepdims=True)
        out = contract(weights.astype(bf16), kv, 1, 0)*(1.0/total)
        logs = jnp.where(lane == head, top + jnp.log2(total), logs)
        if head % 2 == 0:
            held = pltpu.roll(out, VDIM, 1)
        else:
            start = (head//2)*LANES
            o_ref[0, :, start:start+LANES] = jnp.where(lane < VDIM, held, out).astype(bf16)
    lse_ref[0] = logs

def attention_forward(query, kv, rotary, table, limits, heads):
    seqs, rows, _ = query.shape
    keys = kv.shape[1]
    whole = lambda *dims: pl.BlockSpec((1,)+dims, lambda s: (s,)+(0,)*len(dims))
    return pl.pallas_call(
        functools.partial(forward_kernel, heads),
        grid=(seqs,),
        in_specs=[whole(*query.shape[1:]), whole(*kv.shape[1:]), whole(*rotary.shape[1:]),
                  pl.BlockSpec(table.shape, lambda s:(0,0,0)), whole(*limits.shape[1:])],
        out_specs=[whole(rows, heads*VDIM), whole(rows, LANES)],
        out_shape=[jax.ShapeDtypeStruct((seqs,rows,heads*VDIM),bf16), jax.ShapeDtypeStruct((seqs,rows,LANES),f32)],
        scratch_shapes=[pltpu.VMEM((rows,keys),f32)],
        compiler_params=pltpu.CompilerParams(vmem_limit_bytes=50*1024*1024),
        cost_estimate=pl.CostEstimate(flops=seqs*heads*rows*keys*4*LANES, bytes_accessed=12_000_000, transcendentals=seqs*heads*rows*keys),
    )(query, kv, rotary, table, limits)

def backward_kernel(heads, q_ref, kv_ref, rotary_ref, table_ref, limit_ref, lse_ref, go_ref, gq_ref, gkv_ref, gkr_ref, bias_ref):
    keys, rows = bias_ref.shape
    place = lax.broadcasted_iota(jnp.int32, (keys, rows), 0)
    inside = (place >= limit_ref[0, 0:1, :]) & (place <= limit_ref[0, 1:2, :])
    bias_ref[...] = jnp.where(inside, 0.0, big_negative)
    lane = lax.broadcasted_iota(jnp.int32, (rows, LANES), 1)
    key_lane = lax.broadcasted_iota(jnp.int32, (keys, LANES), 1)
    logs = lse_ref[0].T
    grad_rotary = jnp.zeros((keys, LANES), f32)
    for head in range(heads):
        query = padded_query(q_ref, table_ref, head)
        kv = kv_ref[0, :, head*LANES:(head+1)*LANES]
        key = jnp.where(key_lane < NOPE, kv, rotary_ref[0])
        start = (head//2)*LANES
        go = go_ref[0, :, start:start+LANES].astype(f32)
        if head % 2 == 0:
            go = pltpu.roll(go, VDIM, 1)
        go = jnp.where(lane < VDIM, 0.0, go).astype(bf16)
        scores = contract(key, query, 1, 1)*(score_scale*log2e) + bias_ref[...]
        prob = jnp.exp2(scores - logs[head:head+1, :])
        grad_prob = contract(kv, go, 1, 1)
        grad_value = contract(prob.astype(bf16), go, 1, 0)
        mixed = jnp.sum(prob*grad_prob, axis=0, keepdims=True)
        grad_scores = (prob*(grad_prob - mixed)).astype(bf16)
        grad_key = contract(grad_scores, query, 1, 0)*score_scale
        grad_rotary = grad_rotary + grad_key
        gkv_ref[0, :, head*LANES:(head+1)*LANES] = jnp.where(key_lane < NOPE, grad_key, grad_value).astype(bf16)
        grad_query = contract(key, grad_scores, 0, 0).T*score_scale
        grad_query = turned(grad_query, table_ref[0], -table_ref[1], -table_ref[2])
        gq_ref[0, :, head*HEAD:(head+1)*HEAD] = grad_query[:, :HEAD].astype(bf16)
    gkr_ref[0] = grad_rotary

def attention_backward(query, kv, rotary, table, limits, lse, go, heads):
    seqs, rows, _ = query.shape
    keys = kv.shape[1]
    whole = lambda *dims: pl.BlockSpec((1,)+dims, lambda s: (s,)+(0,)*len(dims))
    return pl.pallas_call(
        functools.partial(backward_kernel, heads),
        grid=(seqs,),
        in_specs=[whole(*query.shape[1:]), whole(*kv.shape[1:]), whole(*rotary.shape[1:]),
                  pl.BlockSpec(table.shape, lambda s:(0,0,0)), whole(*limits.shape[1:]), whole(*lse.shape[1:]), whole(*go.shape[1:])],
        out_specs=[whole(rows, heads*HEAD), whole(keys, heads*LANES), whole(keys, LANES)],
        out_shape=[jax.ShapeDtypeStruct((seqs,rows,heads*HEAD),bf16), jax.ShapeDtypeStruct((seqs,keys,heads*LANES),bf16), jax.ShapeDtypeStruct((seqs,keys,LANES),f32)],
        scratch_shapes=[pltpu.VMEM((keys,rows),f32)],
        compiler_params=pltpu.CompilerParams(vmem_limit_bytes=58*1024*1024),
        cost_estimate=pl.CostEstimate(flops=seqs*heads*rows*keys*10*LANES, bytes_accessed=20_000_000, transcendentals=seqs*heads*rows*keys),
    )(query, kv, rotary, table, limits, lse, go)


def weights_kernel(n_group, n_piece, *refs):
    refs = list(refs)

    def take(count):
        return [refs.pop(0) for _ in range(count)]

    tokens = [take(n_piece) for _ in range(n_group)]
    grads = [take(n_piece) for _ in range(n_group)]
    kept = [take(3) for _ in range(n_group)]
    (out,) = refs
    down = gate = up = 0.0
    for group in range(n_group):
        token = jnp.concatenate([piece[...] for piece in tokens[group]], axis=0)
        grad = jnp.concatenate([piece[...] for piece in grads[group]], axis=0)
        hidden, grad_gate, grad_up = kept[group]
        down = down + contract(hidden[...], grad, 1, 0)
        gate = gate + contract(grad_gate[...], token, 1, 0)
        up = up + contract(grad_up[...], token, 1, 0)
    units = gate.shape[0]
    out[0, :units] = gate.astype(bf16)
    out[0, units : 2 * units] = up.astype(bf16)
    out[0, 2 * units :] = down.astype(bf16)


def ffn_weight_grads(tokens, grads, kept):
    n_group, n_piece = len(tokens), len(tokens[0])
    rows, width = tokens[0][0].shape
    units = kept[0][0].shape[0]
    step = width // 4

    def column(height):
        return pl.BlockSpec((height, step), lambda i: (0, i))

    whole = pl.BlockSpec(kept[0][0].shape, lambda i: (0, 0))
    flat = [piece for group in tokens for piece in group]
    flat += [piece for group in grads for piece in group]
    total = rows * n_piece * n_group
    return pl.pallas_call(
        functools.partial(weights_kernel, n_group, n_piece),
        grid=(width // step,),
        in_specs=[column(rows)] * len(flat) + [whole] * (3 * n_group),
        out_specs=pl.BlockSpec((1, 3 * units, step), lambda i: (i % 2, 0, i // 2)),
        out_shape=jax.ShapeDtypeStruct((2, 3 * units, width // 2), bf16),
        compiler_params=pltpu.CompilerParams(vmem_limit_bytes=48 * MIB),
        cost_estimate=pl.CostEstimate(
            flops=6 * total * width * units, bytes_accessed=33_000_000, transcendentals=0
        ),
    )(*flat, *[array for group in kept for array in group])


def group_place():
    return (lax.axis_index("shard") & 1) * 2 + (lax.axis_index("ctx") & 1)


def by_place(write):
    me = group_place()
    for place in range(4):

        @pl.when(me == place)
        def _(place=place):
            write(place)


def join_kernel(*refs):
    length = refs[0].shape[1]
    out_ref = refs[-1]

    def write(me):
        for k in range(4):
            block = me ^ k
            out_ref[:, block * length : (block + 1) * length] = refs[k][...]

    by_place(write)


def join_columns(pieces):
    height, length = pieces[0].shape
    return pl.pallas_call(
        join_kernel,
        out_shape=jax.ShapeDtypeStruct((height, 4 * length), pieces[0].dtype),
        compiler_params=pltpu.CompilerParams(vmem_limit_bytes=16 * MIB),
        cost_estimate=pl.CostEstimate(
            flops=0, bytes_accessed=16 * pieces[0].size, transcendentals=0
        ),
    )(*pieces)


def place_kernel(*refs):
    pieces, (gate_ref, up_ref, down_ref) = refs[:4], refs[4:]
    height = pieces[0].shape[0] // 3

    def write(me):
        for k in range(4):
            rows = slice((me ^ k) * height, ((me ^ k) + 1) * height)
            gate_ref[:, rows] = pieces[k][:height].astype(f32).T
            up_ref[:, rows] = pieces[k][height : 2 * height].astype(f32).T
            down_ref[rows, :] = pieces[k][2 * height :].astype(f32)

    by_place(write)


def place_rows(pieces):
    height, length = pieces[0].shape
    total = 4 * height // 3
    inner = jax.ShapeDtypeStruct((length, total), f32)
    return pl.pallas_call(
        place_kernel,
        out_shape=[inner, inner, jax.ShapeDtypeStruct((total, length), f32)],
        compiler_params=pltpu.CompilerParams(vmem_limit_bytes=40 * MIB),
        cost_estimate=pl.CostEstimate(
            flops=0, bytes_accessed=24 * pieces[0].size, transcendentals=0
        ),
    )(*pieces)


def split_kernel(in_ref, out_ref):
    length = out_ref.shape[2]
    for i in range(4):
        out_ref[i] = in_ref[:, i * length : (i + 1) * length]


def split_columns(values):
    height, length = values.shape
    return pl.pallas_call(
        split_kernel,
        out_shape=jax.ShapeDtypeStruct((4, height, length // 4), bf16),
        compiler_params=pltpu.CompilerParams(vmem_limit_bytes=24 * MIB),
        cost_estimate=pl.CostEstimate(flops=0, bytes_accessed=4 * values.size, transcendentals=0),
    )(values)


def exchange_group(parts):
    me = group_place()
    pieces = [lax.dynamic_index_in_dim(parts, me, 0, False)]
    size = lax.axis_size("ctx")
    for k in range(1, 4):
        send = lax.dynamic_index_in_dim(parts, me ^ k, 0, False)
        pairs = [
            (i * size + j, (i ^ (k >> 1)) * size + (j ^ (k & 1)))
            for i in range(lax.axis_size("shard"))
            for j in range(size)
        ]
        pieces.append(lax.ppermute(send, ("shard", "ctx"), pairs))
    return pieces


def block_sized():
    return lax.axis_size("shard") == 2 and lax.axis_size("ctx") == 4


def hidden_pieces(weights):
    parts = [weight.reshape(4, -1, weight.shape[1]) for weight in weights]
    return exchange_group(jnp.concatenate(parts, axis=1))


def far_groups():
    size = lax.axis_size("ctx")
    return [list(range(first, size, 2)) for first in range(2)]


def hidden_gather(joined):
    return lax.all_gather(joined, "ctx", axis_index_groups=far_groups(), axis=0)


def hidden_rows(whole):
    length, height = whole.shape[2] // 2, whole.shape[1] // 3
    weights = []
    for w in range(3):
        rows = whole[:, w * height : (w + 1) * height]
        blocks = [rows[far, :, i * length : (i + 1) * length] for i in range(2) for far in range(2)]
        weights.append(jnp.concatenate(blocks, axis=1))
    return weights


def hidden_rows_plain(weight):
    whole = lax.all_gather(weight, ("shard", "ctx"), axis=1, tiled=True)
    height = whole.shape[0] // 4
    return lax.dynamic_slice_in_dim(whole, group_place() * height, height, 0)


def hidden_grad_plain(grad):
    length = grad.shape[2] // 2
    blocks = [grad[far, :, i * length : (i + 1) * length] for i in range(2) for far in range(2)]
    grad = jnp.concatenate(blocks, axis=1)
    whole = jnp.zeros((4 * grad.shape[0], grad.shape[1]), bf16)
    whole = lax.dynamic_update_slice_in_dim(whole, grad, group_place() * grad.shape[0], 0)
    whole = lax.psum_scatter(whole, ("shard", "ctx"), scatter_dimension=1, tiled=True)
    return whole.astype(f32)


def on_device(
    hidden_in,
    cotangent,
    doc_lengths,
    attn_gain,
    q_gain,
    kv_gain,
    ffn_gain,
    q_down,
    kv_down,
    q_up,
    kv_up,
    out_proj,
    gate_proj,
    up_proj,
    down_proj,
):
    seqs, piece, width = hidden_in.shape
    n_shard, n_ctx, n_tp = lax.axis_size("shard"), lax.axis_size("ctx"), lax.axis_size("tp")
    rank = lax.axis_index("tp")
    low_bit = (rank & 1) == 1
    rows = seqs * piece
    chunk_rows = rows // n_tp
    seq_len = piece * n_ctx
    offset = lax.axis_index("ctx") * piece
    q_part, kv_part = QRANK // n_tp, (KVRANK + ROPE) // n_tp
    part = q_part + kv_part
    block = q_down.shape[0]
    n_gain = 2 * attn_gain.shape[0] + q_gain.shape[0] + kv_gain.shape[0]

    gain_row = jnp.concatenate([attn_gain, ffn_gain, q_gain, kv_gain])
    n_blocks = n_shard * n_ctx * n_tp
    everywhere = ("shard", "ctx", "tp")
    small = jnp.stack(
        [
            jnp.concatenate(
                [
                    q_down[:, i * q_part : (i + 1) * q_part],
                    kv_down[:, i * kv_part : (i + 1) * kv_part],
                ],
                axis=1,
            )
            for i in range(n_tp)
        ]
    )
    small = jnp.broadcast_to(small[None], (n_ctx,) + small.shape)
    small = lax.all_to_all(small.reshape(n_ctx * n_tp, block, part), ("ctx", "tp"), 0, 0)
    gains = lax.all_to_all(
        after(jnp.broadcast_to(gain_row[None, None], (n_blocks, 1, n_gain)), small), everywhere, 0, 0
    )
    gains = gains[:, 0].astype(f32)
    cut = attn_gain.shape[0]
    gain_attn = gains[:, :cut].reshape(1, -1)
    gain_ffn = gains[:, cut : 2 * cut].reshape(1, -1)
    gain_query = gains[:, 2 * cut : 2 * cut + q_gain.shape[0]].reshape(1, -1)
    gain_latent = gains[:, 2 * cut + q_gain.shape[0] :].reshape(1, -1)

    down_part = gather_shard(small.reshape(-1, part), 0)
    out_full = lax.all_gather(after(out_proj, small), ("shard", "ctx"), axis=1, tiled=True)
    hidden_weights = (gate_proj.T, up_proj.T, down_proj)
    if block_sized():
        pieces = hidden_pieces((after(gate_proj.T, small),) + hidden_weights[1:])
        hidden_joined = join_columns(pieces)
    else:
        gate_full, upward_full, down_full = map(hidden_rows_plain, hidden_weights)
        hidden_joined = gate_full

    up_query = gather_ctx(after(q_up, down_part))
    up_latent = gather_ctx(after(kv_up, down_part))


    heads = q_up.shape[1] // HEAD
    positions = offset + jnp.arange(piece, dtype=jnp.int32)
    cosine_here, sine_here = rope_tables(positions)
    docs = doc_lengths.shape[1]
    ends = jnp.stack([jnp.sum(doc_lengths[:, : i + 1], axis=1) for i in range(docs)], axis=1)
    starts = jnp.max(
        jnp.where(positions[None, :, None] >= ends[:, None, :], ends[:, None, :], 0), axis=-1
    )
    limits = jnp.stack([starts, jnp.broadcast_to(positions[None], starts.shape)], axis=1)
    cosine, sine = cosine_here[:, : ROPE // 2], sine_here[:, : ROPE // 2]
    zero, fill = jnp.zeros_like(cosine), jnp.zeros((piece, LANES - HEAD), f32)
    plain = jnp.zeros((piece, NOPE), f32)
    table = jnp.stack(
        [
            jnp.concatenate([plain + 1.0, cosine, cosine, fill], axis=1),
            jnp.concatenate([plain, -sine, zero, fill], axis=1),
            jnp.concatenate([plain, zero, sine, fill], axis=1),
        ]
    )

    stream = hidden_in.astype(f32).reshape(rows, width)
    grad_out = cotangent.astype(f32).reshape(rows, width)
    chunk_start = rank * chunk_rows

    def own_chunk(values):
        return lax.dynamic_slice_in_dim(values, chunk_start, chunk_rows, 0)

    inverse_one = rms_inverse(stream)
    normed_one = stream * inverse_one
    input_low = (normed_one * gain_attn).astype(bf16)
    low_rank = gather_tp(dot(input_low, down_part, ((1,), (0,))))
    up_query = gather_shard(after(up_query.reshape(-1, q_up.shape[1]), low_rank), 0)
    up_latent = gather_shard(after(up_latent.reshape(-1, kv_up.shape[1]), low_rank), 0)
    query_latent = low_rank[:, :, :q_part].transpose(1, 0, 2).reshape(rows, QRANK)
    latent_raw = low_rank[:, :, q_part:].transpose(1, 0, 2).reshape(rows, KVRANK + ROPE)
    inverse_latent = rms_inverse(latent_raw[:, :KVRANK])
    normed_latent = latent_raw[:, :KVRANK] * inverse_latent
    latent_low = (normed_latent * gain_latent).astype(bf16).reshape(seqs, piece, KVRANK)
    rotary_key = rotate(
        latent_raw[:, KVRANK:].reshape(seqs, piece, ROPE), cosine_here, sine_here
    ).astype(bf16)
    keys_here = jnp.concatenate(
        [latent_low, jnp.pad(rotary_key, ((0, 0), (0, 0), (NOPE, LANES - HEAD)))], axis=-1
    )
    half = seqs // 2
    mine = rank & 1
    keys_mine = lax.dynamic_slice_in_dim(keys_here, mine * half, half, 0)
    keys_mine = gather_ctx(after(keys_mine, hidden_joined))
    if block_sized():
        hidden_gathered = hidden_gather(after(hidden_joined, keys_mine))
        gate_full, upward_full, down_full = hidden_rows(hidden_gathered)
    keys_mine = keys_mine.transpose(1, 0, 2, 3).reshape(half, seq_len, KVRANK + LANES)
    keys_all = pair_order(keys_mine, tp_xor(keys_mine, 1), low_bit, 0)
    latent_all, rotary_all = keys_all[..., :KVRANK], keys_all[..., KVRANK:]

    grad_ffn = gather_tokens((res_scale * own_chunk(grad_out)).astype(bf16))

    inverse_query = rms_inverse(query_latent)
    normed_query = query_latent * inverse_query
    query_low = (normed_query * gain_query).astype(bf16)
    key_value = jnp.einsum("slr,rf->slf", latent_all, up_latent, preferred_element_type=f32)
    key_value = key_value.astype(bf16)
    query = dot(query_low, up_query, ((1,), (0,))).reshape(seqs, piece, -1)
    attended_low, log_total = attention_forward(
        query, key_value, rotary_all, table, limits.transpose(0, 2, 1), heads
    )
    attended_low = attended_low.reshape(rows, heads * VDIM)

    attn_out = scatter_tp(
        dot(attended_low, out_full, ((1,), (0,))).reshape(n_tp, chunk_rows, width)
    )
    middle = own_chunk(stream) + res_scale * attn_out
    inverse_two = rms_inverse(middle)
    normed_two = middle * inverse_two
    ffn_own = gather_tokens(
        (normed_two * gain_ffn).astype(bf16), *([hidden_gathered] if block_sized() else [])
    )
    ffn_groups = [ffn_own, swap(ffn_own, "tp", 1)]
    grad_ffn_groups = [grad_ffn, swap(grad_ffn, "tp", 1)]
    ffn_parts, grad_two_parts, kept = [], [], []
    for ffn_low, grad_low in zip(ffn_groups, grad_ffn_groups):
        gate_value = dot(ffn_low, gate_full, ((1,), (1,)))
        up_value = dot(ffn_low, upward_full, ((1,), (1,)))
        sigma = jax.nn.sigmoid(gate_value)
        gate_act = gate_value * sigma
        hidden_low = (gate_act * up_value).astype(bf16)
        grad_hidden = dot(grad_low, down_full, ((1,), (1,)))
        grad_gate = (grad_hidden * up_value * sigma * (1.0 + gate_value * (1.0 - sigma))).astype(
            bf16
        )
        grad_upward = (grad_hidden * gate_act).astype(bf16)
        grad_two_part = dot(grad_gate, gate_full, ((1,), (0,)))
        grad_two_part = grad_two_part + dot(grad_upward, upward_full, ((1,), (0,)))
        grad_two_parts.append(grad_two_part.astype(bf16))
        ffn_parts.append(dot(hidden_low, down_full, ((1,), (0,))).astype(bf16))
        kept.append((hidden_low.T, grad_gate.T, grad_upward.T))

    grad_two = scatter_tokens(scatter_near(*grad_two_parts))
    hidden_grads = ffn_weight_grads(
        [[group] for group in ffn_groups], [[group] for group in grad_ffn_groups], kept
    )
    if block_sized():
        hidden_sums = lax.psum_scatter(
            hidden_grads,
            "ctx",
            scatter_dimension=0,
            axis_index_groups=far_groups(),
        )
    ffn_sum = scatter_near(ffn_parts[0], after(ffn_parts[1], grad_two))
    down_all = gather_tp(after(down_part.T, grad_two)).reshape(-1, width)
    grad_middle = own_chunk(grad_out) + norm_backward(grad_two, normed_two, inverse_two, gain_ffn)
    grad_gain_ffn = jnp.sum(grad_two * normed_two, axis=0)
    grad_attn = after((res_scale * grad_middle).astype(bf16), hidden_grads)
    grad_attn = gather_tp(grad_attn).reshape(rows, width)

    grad_out_w = lax.psum_scatter(
        dot(attended_low, grad_attn, ((0,), (0,))).astype(bf16),
        ("shard", "ctx"),
        scatter_dimension=1,
        tiled=True,
    ).astype(f32)

    grad_attended = dot(grad_attn, out_full, ((1,), (1,))).astype(bf16)
    grad_query, grad_key_value, grad_krope = attention_backward(
        query,
        key_value,
        rotary_all,
        table,
        limits,
        log_total,
        grad_attended.reshape(seqs, piece, -1),
        heads,
    )
    grad_query = grad_query.reshape(rows, heads * HEAD)
    grad_key_value = grad_key_value.reshape(seqs * seq_len, heads * (NOPE + VDIM))

    grad_keys = dot(grad_key_value, up_latent, ((1,), (1,))).astype(bf16)
    grad_keys = jnp.concatenate(
        [grad_keys.reshape(seqs, seq_len, KVRANK), grad_krope.astype(bf16)], axis=-1
    )

    def add_near(values):
        keep = lax.dynamic_slice_in_dim(values, mine * half, half, 0)
        send = lax.dynamic_slice_in_dim(values, (1 - mine) * half, half, 0)
        return keep.astype(f32) + tp_xor(send, 1).astype(f32)

    grad_keys = add_near(grad_keys).astype(bf16)
    grad_keys = scatter_ctx(
        grad_keys.reshape(half, n_ctx, piece, KVRANK + LANES).transpose(1, 0, 2, 3)
    )
    grad_pre_query = dot(grad_query, up_query, ((1,), (1,))).astype(bf16)
    grad_pre_query = add_near(grad_pre_query.reshape(seqs, piece, QRANK))
    ffn_sum = scatter_step(scatter_begin(ffn_sum), 2)
    grad_low = jnp.concatenate([grad_pre_query, grad_keys], axis=-1).astype(bf16)
    grad_low = after(grad_low, *ffn_sum)
    grad_low = (grad_low.astype(f32) + tp_xor(grad_low, 2).astype(f32)).astype(bf16)
    grad_low = pair_order(grad_low, tp_xor(grad_low, 1), low_bit, 0)
    ffn_sum = scatter_step(ffn_sum, 1)
    grad_low = after(grad_low.reshape(rows, QRANK + KVRANK + LANES), *ffn_sum)
    ffn_sum = scatter_end(scatter_step(ffn_sum, 0))
    hidden_back = []
    if block_sized():
        hidden_back = exchange_group(split_columns(hidden_sums))
        down_all = after(down_all, *hidden_back)
    grad_low = grad_low.astype(f32)

    grad_out_query, grad_out_latent = grad_low[:, :QRANK], grad_low[:, QRANK : QRANK + KVRANK]
    grad_query_latent = norm_backward(grad_out_query, normed_query, inverse_query, gain_query)
    grad_compressed = norm_backward(grad_out_latent, normed_latent, inverse_latent, gain_latent)
    grad_gain_query = jnp.sum(own_chunk(grad_out_query * normed_query), axis=0)
    grad_gain_latent = jnp.sum(own_chunk(grad_out_latent * normed_latent), axis=0)
    grad_rotary = grad_low[:, QRANK + KVRANK + NOPE : QRANK + KVRANK + HEAD]
    grad_rotary = grad_rotary.reshape(seqs, piece, ROPE)
    grad_rotary = unrotate(grad_rotary, cosine_here, sine_here).reshape(rows, ROPE)
    grad_query_latent = grad_query_latent.astype(bf16)
    grad_latent_raw = jnp.concatenate([grad_compressed, grad_rotary], axis=-1).astype(bf16)

    own_query, own_latent = own_chunk(grad_query_latent), own_chunk(grad_latent_raw)
    grad_parts = [
        part_of[:, i * length : (i + 1) * length]
        for i in range(n_tp)
        for part_of, length in ((own_query, q_part), (own_latent, kv_part))
    ]
    grad_pre_one = dot(jnp.concatenate(grad_parts, axis=1), down_all, ((1,), (0,)))
    normed_own = own_chunk(normed_one)
    grad_input = grad_middle + norm_backward(
        grad_pre_one, normed_own, own_chunk(inverse_one), gain_attn
    )
    grad_gain_attn = jnp.sum(grad_pre_one * normed_own, axis=0)
    grad_input = round_low(grad_input).astype(bf16)
    grad_input = gather_tp(grad_input).astype(f32)

    grad_part = jnp.concatenate(
        [
            lax.dynamic_slice_in_dim(grad_query_latent, rank * q_part, q_part, 1),
            lax.dynamic_slice_in_dim(grad_latent_raw, rank * kv_part, kv_part, 1),
        ],
        axis=1,
    )
    grad_small = dot(input_low, grad_part, ((0,), (0,)))
    grad_half = scatter_shard(grad_small, 0)
    grad_small = scatter_ctx(grad_half.reshape(n_ctx, n_tp, block, part))
    grad_small = exchange_tp(grad_small.astype(bf16)).astype(f32).transpose(1, 0, 2)
    grad_down_query = grad_small[:, :, :q_part].reshape(block, QRANK)
    grad_down_latent = grad_small[:, :, q_part:].reshape(block, KVRANK + ROPE)
    grad_gains = jnp.concatenate(
        [
            grad_gain_attn.reshape(n_blocks, -1),
            grad_gain_ffn.reshape(n_blocks, -1),
            grad_gain_query.reshape(n_blocks, -1),
            grad_gain_latent.reshape(n_blocks, -1),
        ],
        axis=1,
    )
    grad_gains = lax.all_to_all(grad_gains[:, None], everywhere, 0, 0)
    grad_gains = jnp.sum(grad_gains[:, 0], axis=0)

    output = round_low(middle + res_scale * ffn_sum)
    output = gather_tp(output.astype(bf16)).astype(f32)

    def rows_grad(grad):
        mine = scatter_shard(grad, 0)
        return scatter_ctx(mine.reshape(n_ctx, -1, mine.shape[-1]))

    grad_up_query = rows_grad(dot(query_low, grad_query, ((0,), (0,))))
    grad_up_latent = rows_grad(
        dot(latent_all.reshape(-1, KVRANK), grad_key_value, ((0,), (0,)))
    )
    if block_sized():
        grad_gate_w, grad_upward_w, grad_down_w = place_rows(hidden_back)
    else:
        units = hidden_grads.shape[1] // 3
        split = [hidden_grads[:, i * units : (i + 1) * units] for i in range(3)]
        grad_gate_w, grad_upward_w, grad_down_w = map(hidden_grad_plain, split)
        grad_gate_w, grad_upward_w = grad_gate_w.T, grad_upward_w.T
    return (
        output.reshape(seqs, piece, width),
        grad_input.reshape(seqs, piece, width),
        grad_gains[:cut],
        grad_gains[2 * cut : 2 * cut + q_gain.shape[0]],
        grad_gains[2 * cut + q_gain.shape[0] :],
        grad_gains[cut : 2 * cut],
        grad_down_query,
        grad_down_latent,
        grad_up_query,
        grad_up_latent,
        grad_out_w,
        grad_gate_w,
        grad_upward_w,
        grad_down_w,
    )


def solution(mesh):
    all_axes = ("shard", "ctx", "tp")
    tokens, vector, square = P("shard", "ctx", None), P(all_axes), P(all_axes, None)
    inner, outer = P(("shard", "ctx"), "tp"), P("tp", ("shard", "ctx"))
    weights = (
        vector,
        vector,
        vector,
        vector,
        square,
        square,
        inner,
        inner,
        outer,
        inner,
        inner,
        outer,
    )
    return jax.shard_map(
        on_device,
        mesh=mesh,
        in_specs=(tokens, tokens, P("shard", None)) + weights,
        out_specs=(tokens, tokens) + weights,
        check_vma=False,
    )
```

```python
import functools
import math

import jax
import jax.numpy as jnp
from jax import lax
from jax.experimental import pallas as pl
from jax.experimental.pallas import tpu as pltpu
from jax.sharding import PartitionSpec as P

NOPE = 64
ROPE = 32
VDIM = 64
KVRANK = 256
QRANK = 768
LANES = 128
HEAD = NOPE + ROPE
score_scale = 1.0 / math.sqrt(HEAD)
log2e = 1.0 / math.log(2.0)
MIB = 1024 * 1024

eps = 1e-05
res_scale = 1.4 / math.sqrt(62.0)
big_negative = -1e30
f32 = jnp.float32
bf16 = jnp.bfloat16


def rope_tables(positions):
    half = ROPE // 2
    inverse = jnp.exp(-math.log(10000.0) * jnp.arange(half, dtype=f32) * 2.0 / ROPE)
    angles = positions.astype(f32)[:, None] * inverse[None, :]
    angles = jnp.concatenate([angles, angles], axis=-1)
    return (jnp.cos(angles), jnp.sin(angles))


def rotate_half(values):
    half = values.shape[-1] // 2
    return jnp.concatenate([-values[..., half:], values[..., :half]], axis=-1)


def rotate(values, cosine, sine):
    return values * cosine + rotate_half(values) * sine


def unrotate(grads, cosine, sine):
    return grads * cosine - rotate_half(grads) * sine


def rms_inverse(values):
    return lax.rsqrt(jnp.mean(values * values, axis=-1, keepdims=True) + eps)


def norm_backward(grad_out, normed, inverse_rms, gain):
    scaled = grad_out * gain
    return inverse_rms * (scaled - normed * jnp.mean(scaled * normed, axis=-1, keepdims=True))


def dot(left, right, dims):
    return lax.dot_general(left, right, (dims, ((), ())), preferred_element_type=f32)


def round_low(values):
    return lax.reduce_precision(values, 8, 7)


def tp_xor(values, mask):
    size = lax.axis_size("tp")
    return lax.ppermute(values, "tp", [(i, i ^ mask) for i in range(size)])


def from_ctx(values, shift):
    size = lax.axis_size("ctx")
    return lax.ppermute(values, "ctx", [((i + shift) % size, i) for i in range(size)])


def exchange_ctx(parts):
    size = lax.axis_size("ctx")
    me = lax.axis_index("ctx")
    came = [lax.dynamic_index_in_dim(parts, me, 0, False)]
    for shift in range(1, size):
        send = lax.dynamic_index_in_dim(parts, lax.rem(me + shift, size), 0, False)
        came.append(lax.ppermute(send, "ctx", [(i, (i + shift) % size) for i in range(size)]))
    return came


def placed(pieces, places):
    whole = jnp.zeros((len(pieces),) + pieces[0].shape, pieces[0].dtype)
    for piece, place in zip(pieces, places):
        whole = lax.dynamic_update_index_in_dim(whole, piece, place, 0)
    return whole


def gather_ctx(values):
    size = lax.axis_size("ctx")
    me = lax.axis_index("ctx")
    pieces = [values] + [from_ctx(values, shift) for shift in range(1, size)]
    return placed(pieces, [lax.rem(me + shift, size) for shift in range(size)])


def exchange_tp(parts):
    rank = lax.axis_index("tp")
    size = lax.axis_size("tp")
    pieces = [lax.dynamic_index_in_dim(parts, rank, 0, False)]
    for mask in range(1, size):
        pieces.append(tp_xor(lax.dynamic_index_in_dim(parts, rank ^ mask, 0, False), mask))
    return placed(pieces, [rank ^ mask for mask in range(size)])


def pair_order(own, other, second, axis):
    return jnp.concatenate(
        [jnp.where(second, other, own), jnp.where(second, own, other)], axis=axis
    )


def gather_shard(values, axis):
    if lax.axis_size("shard") == 2:
        other = lax.ppermute(values, "shard", [(0, 1), (1, 0)])
        return pair_order(values, other, lax.axis_index("shard") == 1, axis)
    return lax.all_gather(values, "shard", axis=axis, tiled=True)


def scatter_shard(values, axis):
    size = lax.axis_size("shard")
    if size == 2:
        length = values.shape[axis] // 2
        low = lax.slice_in_dim(values, 0, length, axis=axis)
        high = lax.slice_in_dim(values, length, 2 * length, axis=axis)
        second = lax.axis_index("shard") == 1
        keep = jnp.where(second, high, low)
        send = jnp.where(second, low, high).astype(bf16)
        return keep + lax.ppermute(send, "shard", [(0, 1), (1, 0)]).astype(f32)
    return lax.psum_scatter(
        values.astype(bf16), "shard", scatter_dimension=axis, tiled=True
    ).astype(f32)


def scatter_ctx(values):
    me = lax.axis_index("ctx")
    own = lax.dynamic_index_in_dim(values, me, 0, False).astype(f32)
    return sum((piece.astype(f32) for piece in exchange_ctx(values.astype(bf16))[1:]), own)


def gather_tp(chunk):
    rank = lax.axis_index("tp")
    low_bit, high_bit = (rank & 1) == 1, (rank >> 1) == 1
    other = tp_xor(chunk, 2)
    pair = jnp.stack([jnp.where(high_bit, other, chunk), jnp.where(high_bit, chunk, other)])
    across = tp_xor(pair, 1)
    both = jnp.stack(
        [jnp.where(low_bit, across, pair), jnp.where(low_bit, pair, across)], axis=1
    )
    return both.reshape((4,) + chunk.shape)


def scatter_tp(partial_sum, *earlier):
    rank = lax.axis_index("tp")
    low_bit, high_bit = (rank & 1) == 1, (rank >> 1) == 1
    parts = partial_sum.reshape((2, 2) + partial_sum.shape[1:])
    keep = jnp.where(low_bit, parts[:, 1], parts[:, 0])
    send = jnp.where(low_bit, parts[:, 0], parts[:, 1]).astype(bf16)
    summed = keep + tp_xor(send, 1).astype(f32)
    keep = jnp.where(high_bit, summed[1], summed[0])
    send = jnp.where(high_bit, summed[0], summed[1]).astype(bf16)
    if earlier:
        send = after(send, *earlier)
    return keep + tp_xor(send, 2).astype(f32)


def after_kernel(*refs):
    pass


def after(values, *earlier):
    anywhere = pl.BlockSpec(memory_space=pl.ANY)
    return pl.pallas_call(
        after_kernel,
        in_specs=[anywhere] * (1 + len(earlier)),
        out_specs=anywhere,
        out_shape=jax.ShapeDtypeStruct(values.shape, values.dtype),
        input_output_aliases={0: 0},
        cost_estimate=pl.CostEstimate(flops=0, bytes_accessed=0, transcendentals=0),
    )(values, *earlier)


def swap(values, axis, mask):
    size = lax.axis_size(axis)
    return lax.ppermute(values, axis, [(i, i ^ mask) for i in range(size)])


WAYS = {"x": ("tp", 2, 0), "y": ("shard", 1, 1), "z": ("ctx", 1, 2)}
ORDERS = (("x", "y", "z"), ("y", "z", "x"), ("z", "x", "y"))


def column_cuts(width):
    tiles = width // LANES
    cuts = [0, (tiles + 2) // 3, (tiles + 2) // 3 + (tiles + 1) // 3, tiles]
    return [cut * LANES for cut in cuts]


def gather_tokens(chunk, *earlier):
    cuts = column_cuts(chunk.shape[1])
    parts = [
        chunk[None, None, None, :, cuts[i] : cuts[i + 1]] for i in range(len(ORDERS))
    ]
    for step in range(3):
        if step == 1 and earlier:
            parts[0] = after(parts[0], *earlier)
        for i, order in enumerate(ORDERS):
            axis, mask, dim = WAYS[order[step]]
            parts[i] = jnp.concatenate([parts[i], swap(parts[i], axis, mask)], axis=dim)
    whole = jnp.concatenate(parts, axis=-1)
    return whole.reshape(-1, chunk.shape[1])


def scatter_near(own, other):
    return (own.astype(f32) + swap(other, "tp", 1).astype(f32)).astype(bf16)


def scatter_step(parts, step):
    result = []
    for part, order in zip(parts, ORDERS):
        axis, mask, dim = WAYS[order[step]]
        keep = lax.slice_in_dim(part, 0, 1, axis=dim)
        send = lax.slice_in_dim(part, 1, 2, axis=dim)
        summed = keep.astype(f32) + swap(send, axis, mask).astype(f32)
        result.append(summed.astype(bf16) if step else summed)
    return result


def scatter_begin(total):
    cuts = column_cuts(total.shape[1])
    total = total.reshape(2, 2, 2, -1, total.shape[1])
    return [total[..., cuts[i] : cuts[i + 1]] for i in range(len(ORDERS))]


def scatter_end(parts):
    whole = jnp.concatenate(parts, axis=-1)
    return whole.reshape(-1, whole.shape[-1])


def scatter_tokens(total):
    parts = scatter_begin(total)
    for step in reversed(range(3)):
        parts = scatter_step(parts, step)
    return scatter_end(parts)


def contract(left,right,ld,rd):
    return lax.dot_general(left,right,(((ld,),(rd,)),((),())),preferred_element_type=f32)

def turned(values, keep, ahead, behind):
    return values*keep + pltpu.roll(values, LANES-ROPE//2, 1)*ahead + pltpu.roll(values, ROPE//2, 1)*behind

def padded_query(q_ref, table_ref, head):
    raw = q_ref[0, :, head*HEAD:(head+1)*HEAD]
    raw = jnp.concatenate([raw, jnp.zeros((raw.shape[0], LANES-HEAD), f32)], axis=1)
    return turned(raw, table_ref[0], table_ref[1], table_ref[2]).astype(bf16)

def forward_kernel(heads, q_ref, kv_ref, rotary_ref, table_ref, limit_ref, o_ref, lse_ref, bias_ref):
    rows, keys = bias_ref.shape
    place = lax.broadcasted_iota(jnp.int32, (rows, keys), 1)
    inside = (place >= limit_ref[0, :, 0:1]) & (place <= limit_ref[0, :, 1:2])
    bias_ref[...] = jnp.where(inside, 0.0, big_negative)
    lane = lax.broadcasted_iota(jnp.int32, (rows, LANES), 1)
    key_lane = lax.broadcasted_iota(jnp.int32, (keys, LANES), 1)
    logs = jnp.zeros((rows, LANES), f32)
    held = None
    for head in range(heads):
        query = padded_query(q_ref, table_ref, head)
        kv = kv_ref[0, :, head*LANES:(head+1)*LANES]
        key = jnp.where(key_lane < NOPE, kv, rotary_ref[0])
        scores = contract(query, key, 1, 1)*(score_scale*log2e) + bias_ref[...]
        top = jnp.max(scores, axis=1, keepdims=True)
        weights = jnp.exp2(scores - top)
        total = jnp.sum(weights, axis=1, keepdims=True)
        out = contract(weights.astype(bf16), kv, 1, 0)*(1.0/total)
        logs = jnp.where(lane == head, top + jnp.log2(total), logs)
        if head % 2 == 0:
            held = pltpu.roll(out, VDIM, 1)
        else:
            start = (head//2)*LANES
            o_ref[0, :, start:start+LANES] = jnp.where(lane < VDIM, held, out).astype(bf16)
    lse_ref[0] = logs

def attention_forward(query, kv, rotary, table, limits, heads):
    seqs, rows, _ = query.shape
    keys = kv.shape[1]
    whole = lambda *dims: pl.BlockSpec((1,)+dims, lambda s: (s,)+(0,)*len(dims))
    return pl.pallas_call(
        functools.partial(forward_kernel, heads),
        grid=(seqs,),
        in_specs=[whole(*query.shape[1:]), whole(*kv.shape[1:]), whole(*rotary.shape[1:]),
                  pl.BlockSpec(table.shape, lambda s:(0,0,0)), whole(*limits.shape[1:])],
        out_specs=[whole(rows, heads*VDIM), whole(rows, LANES)],
        out_shape=[jax.ShapeDtypeStruct((seqs,rows,heads*VDIM),bf16), jax.ShapeDtypeStruct((seqs,rows,LANES),f32)],
        scratch_shapes=[pltpu.VMEM((rows,keys),f32)],
        compiler_params=pltpu.CompilerParams(vmem_limit_bytes=50*1024*1024),
        cost_estimate=pl.CostEstimate(flops=seqs*heads*rows*keys*4*LANES, bytes_accessed=12_000_000, transcendentals=seqs*heads*rows*keys),
    )(query, kv, rotary, table, limits)

def backward_kernel(heads, q_ref, kv_ref, rotary_ref, table_ref, limit_ref, lse_ref, go_ref, gq_ref, gkv_ref, gkr_ref, bias_ref):
    keys, rows = bias_ref.shape
    place = lax.broadcasted_iota(jnp.int32, (keys, rows), 0)
    inside = (place >= limit_ref[0, 0:1, :]) & (place <= limit_ref[0, 1:2, :])
    bias_ref[...] = jnp.where(inside, 0.0, big_negative)
    lane = lax.broadcasted_iota(jnp.int32, (rows, LANES), 1)
    key_lane = lax.broadcasted_iota(jnp.int32, (keys, LANES), 1)
    logs = lse_ref[0].T
    grad_rotary = jnp.zeros((keys, LANES), f32)
    for head in range(heads):
        query = padded_query(q_ref, table_ref, head)
        kv = kv_ref[0, :, head*LANES:(head+1)*LANES]
        key = jnp.where(key_lane < NOPE, kv, rotary_ref[0])
        start = (head//2)*LANES
        go = go_ref[0, :, start:start+LANES].astype(f32)
        if head % 2 == 0:
            go = pltpu.roll(go, VDIM, 1)
        go = jnp.where(lane < VDIM, 0.0, go).astype(bf16)
        scores = contract(key, query, 1, 1)*(score_scale*log2e) + bias_ref[...]
        prob = jnp.exp2(scores - logs[head:head+1, :])
        grad_prob = contract(kv, go, 1, 1)
        grad_value = contract(prob.astype(bf16), go, 1, 0)
        mixed = jnp.sum(prob*grad_prob, axis=0, keepdims=True)
        grad_scores = (prob*(grad_prob - mixed)).astype(bf16)
        grad_key = contract(grad_scores, query, 1, 0)*score_scale
        grad_rotary = grad_rotary + grad_key
        gkv_ref[0, :, head*LANES:(head+1)*LANES] = jnp.where(key_lane < NOPE, grad_key, grad_value).astype(bf16)
        grad_query = contract(key, grad_scores, 0, 0).T*score_scale
        grad_query = turned(grad_query, table_ref[0], -table_ref[1], -table_ref[2])
        gq_ref[0, :, head*HEAD:(head+1)*HEAD] = grad_query[:, :HEAD].astype(bf16)
    gkr_ref[0] = grad_rotary

def attention_backward(query, kv, rotary, table, limits, lse, go, heads):
    seqs, rows, _ = query.shape
    keys = kv.shape[1]
    whole = lambda *dims: pl.BlockSpec((1,)+dims, lambda s: (s,)+(0,)*len(dims))
    return pl.pallas_call(
        functools.partial(backward_kernel, heads),
        grid=(seqs,),
        in_specs=[whole(*query.shape[1:]), whole(*kv.shape[1:]), whole(*rotary.shape[1:]),
                  pl.BlockSpec(table.shape, lambda s:(0,0,0)), whole(*limits.shape[1:]), whole(*lse.shape[1:]), whole(*go.shape[1:])],
        out_specs=[whole(rows, heads*HEAD), whole(keys, heads*LANES), whole(keys, LANES)],
        out_shape=[jax.ShapeDtypeStruct((seqs,rows,heads*HEAD),bf16), jax.ShapeDtypeStruct((seqs,keys,heads*LANES),bf16), jax.ShapeDtypeStruct((seqs,keys,LANES),f32)],
        scratch_shapes=[pltpu.VMEM((keys,rows),f32)],
        compiler_params=pltpu.CompilerParams(vmem_limit_bytes=58*1024*1024),
        cost_estimate=pl.CostEstimate(flops=seqs*heads*rows*keys*10*LANES, bytes_accessed=20_000_000, transcendentals=seqs*heads*rows*keys),
    )(query, kv, rotary, table, limits, lse, go)


def weights_kernel(n_group, n_piece, *refs):
    refs = list(refs)

    def take(count):
        return [refs.pop(0) for _ in range(count)]

    tokens = [take(n_piece) for _ in range(n_group)]
    grads = [take(n_piece) for _ in range(n_group)]
    kept = [take(3) for _ in range(n_group)]
    (out,) = refs
    down = gate = up = 0.0
    for group in range(n_group):
        token = jnp.concatenate([piece[...] for piece in tokens[group]], axis=0)
        grad = jnp.concatenate([piece[...] for piece in grads[group]], axis=0)
        hidden, grad_gate, grad_up = kept[group]
        down = down + contract(hidden[...], grad, 1, 0)
        gate = gate + contract(grad_gate[...], token, 1, 0)
        up = up + contract(grad_up[...], token, 1, 0)
    units = gate.shape[0]
    out[0, :units] = gate.astype(bf16)
    out[0, units : 2 * units] = up.astype(bf16)
    out[0, 2 * units :] = down.astype(bf16)


def ffn_weight_grads(tokens, grads, kept):
    n_group, n_piece = len(tokens), len(tokens[0])
    rows, width = tokens[0][0].shape
    units = kept[0][0].shape[0]
    step = width // 4

    def column(height):
        return pl.BlockSpec((height, step), lambda i: (0, i))

    whole = pl.BlockSpec(kept[0][0].shape, lambda i: (0, 0))
    flat = [piece for group in tokens for piece in group]
    flat += [piece for group in grads for piece in group]
    total = rows * n_piece * n_group
    return pl.pallas_call(
        functools.partial(weights_kernel, n_group, n_piece),
        grid=(width // step,),
        in_specs=[column(rows)] * len(flat) + [whole] * (3 * n_group),
        out_specs=pl.BlockSpec((1, 3 * units, step), lambda i: (i % 2, 0, i // 2)),
        out_shape=jax.ShapeDtypeStruct((2, 3 * units, width // 2), bf16),
        compiler_params=pltpu.CompilerParams(vmem_limit_bytes=48 * MIB),
        cost_estimate=pl.CostEstimate(
            flops=6 * total * width * units, bytes_accessed=33_000_000, transcendentals=0
        ),
    )(*flat, *[array for group in kept for array in group])


def group_place():
    return (lax.axis_index("shard") & 1) * 2 + (lax.axis_index("ctx") & 1)


def by_place(write):
    me = group_place()
    for place in range(4):

        @pl.when(me == place)
        def _(place=place):
            write(place)


def join_kernel(*refs):
    length = refs[0].shape[1]
    out_ref = refs[-1]

    def write(me):
        for k in range(4):
            block = me ^ k
            out_ref[:, block * length : (block + 1) * length] = refs[k][...]

    by_place(write)


def join_columns(pieces):
    height, length = pieces[0].shape
    return pl.pallas_call(
        join_kernel,
        out_shape=jax.ShapeDtypeStruct((height, 4 * length), pieces[0].dtype),
        compiler_params=pltpu.CompilerParams(vmem_limit_bytes=16 * MIB),
        cost_estimate=pl.CostEstimate(
            flops=0, bytes_accessed=16 * pieces[0].size, transcendentals=0
        ),
    )(*pieces)


def place_kernel(*refs):
    pieces, (gate_ref, up_ref, down_ref) = refs[:4], refs[4:]
    height = pieces[0].shape[0] // 3

    def write(me):
        for k in range(4):
            rows = slice((me ^ k) * height, ((me ^ k) + 1) * height)
            gate_ref[:, rows] = pieces[k][:height].astype(f32).T
            up_ref[:, rows] = pieces[k][height : 2 * height].astype(f32).T
            down_ref[rows, :] = pieces[k][2 * height :].astype(f32)

    by_place(write)


def place_rows(pieces):
    height, length = pieces[0].shape
    total = 4 * height // 3
    inner = jax.ShapeDtypeStruct((length, total), f32)
    return pl.pallas_call(
        place_kernel,
        out_shape=[inner, inner, jax.ShapeDtypeStruct((total, length), f32)],
        compiler_params=pltpu.CompilerParams(vmem_limit_bytes=40 * MIB),
        cost_estimate=pl.CostEstimate(
            flops=0, bytes_accessed=24 * pieces[0].size, transcendentals=0
        ),
    )(*pieces)


def split_kernel(in_ref, out_ref):
    length = out_ref.shape[2]
    for i in range(4):
        out_ref[i] = in_ref[:, i * length : (i + 1) * length]


def split_columns(values):
    height, length = values.shape
    return pl.pallas_call(
        split_kernel,
        out_shape=jax.ShapeDtypeStruct((4, height, length // 4), bf16),
        compiler_params=pltpu.CompilerParams(vmem_limit_bytes=24 * MIB),
        cost_estimate=pl.CostEstimate(flops=0, bytes_accessed=4 * values.size, transcendentals=0),
    )(values)


def exchange_group(parts):
    me = group_place()
    pieces = [lax.dynamic_index_in_dim(parts, me, 0, False)]
    size = lax.axis_size("ctx")
    for k in range(1, 4):
        send = lax.dynamic_index_in_dim(parts, me ^ k, 0, False)
        pairs = [
            (i * size + j, (i ^ (k >> 1)) * size + (j ^ (k & 1)))
            for i in range(lax.axis_size("shard"))
            for j in range(size)
        ]
        pieces.append(lax.ppermute(send, ("shard", "ctx"), pairs))
    return pieces


def block_sized():
    return lax.axis_size("shard") == 2 and lax.axis_size("ctx") == 4


def hidden_pieces(weights):
    parts = [weight.reshape(4, -1, weight.shape[1]) for weight in weights]
    return exchange_group(jnp.concatenate(parts, axis=1))


def far_groups():
    size = lax.axis_size("ctx")
    return [list(range(first, size, 2)) for first in range(2)]


def hidden_gather(joined):
    return lax.all_gather(joined, "ctx", axis_index_groups=far_groups(), axis=0)


def hidden_rows(whole):
    length, height = whole.shape[2] // 2, whole.shape[1] // 3
    weights = []
    for w in range(3):
        rows = whole[:, w * height : (w + 1) * height]
        blocks = [rows[far, :, i * length : (i + 1) * length] for i in range(2) for far in range(2)]
        weights.append(jnp.concatenate(blocks, axis=1))
    return weights


def hidden_rows_plain(weight):
    whole = lax.all_gather(weight, ("shard", "ctx"), axis=1, tiled=True)
    height = whole.shape[0] // 4
    return lax.dynamic_slice_in_dim(whole, group_place() * height, height, 0)


def hidden_grad_plain(grad):
    length = grad.shape[2] // 2
    blocks = [grad[far, :, i * length : (i + 1) * length] for i in range(2) for far in range(2)]
    grad = jnp.concatenate(blocks, axis=1)
    whole = jnp.zeros((4 * grad.shape[0], grad.shape[1]), bf16)
    whole = lax.dynamic_update_slice_in_dim(whole, grad, group_place() * grad.shape[0], 0)
    whole = lax.psum_scatter(whole, ("shard", "ctx"), scatter_dimension=1, tiled=True)
    return whole.astype(f32)


def on_device(
    hidden_in,
    cotangent,
    doc_lengths,
    attn_gain,
    q_gain,
    kv_gain,
    ffn_gain,
    q_down,
    kv_down,
    q_up,
    kv_up,
    out_proj,
    gate_proj,
    up_proj,
    down_proj,
):
    seqs, piece, width = hidden_in.shape
    n_shard, n_ctx, n_tp = lax.axis_size("shard"), lax.axis_size("ctx"), lax.axis_size("tp")
    rank = lax.axis_index("tp")
    low_bit = (rank & 1) == 1
    rows = seqs * piece
    chunk_rows = rows // n_tp
    seq_len = piece * n_ctx
    offset = lax.axis_index("ctx") * piece
    q_part, kv_part = QRANK // n_tp, (KVRANK + ROPE) // n_tp
    part = q_part + kv_part
    block = q_down.shape[0]
    n_gain = 2 * attn_gain.shape[0] + q_gain.shape[0] + kv_gain.shape[0]

    gain_row = jnp.concatenate([attn_gain, ffn_gain, q_gain, kv_gain])
    n_blocks = n_shard * n_ctx * n_tp
    everywhere = ("shard", "ctx", "tp")
    small = jnp.stack(
        [
            jnp.concatenate(
                [
                    q_down[:, i * q_part : (i + 1) * q_part],
                    kv_down[:, i * kv_part : (i + 1) * kv_part],
                ],
                axis=1,
            )
            for i in range(n_tp)
        ]
    )
    small = jnp.broadcast_to(small[None], (n_ctx,) + small.shape)
    small = lax.all_to_all(small.reshape(n_ctx * n_tp, block, part), ("ctx", "tp"), 0, 0)
    gains = lax.all_to_all(
        after(jnp.broadcast_to(gain_row[None, None], (n_blocks, 1, n_gain)), small), everywhere, 0, 0
    )
    gains = gains[:, 0].astype(f32)
    cut = attn_gain.shape[0]
    gain_attn = gains[:, :cut].reshape(1, -1)
    gain_ffn = gains[:, cut : 2 * cut].reshape(1, -1)
    gain_query = gains[:, 2 * cut : 2 * cut + q_gain.shape[0]].reshape(1, -1)
    gain_latent = gains[:, 2 * cut + q_gain.shape[0] :].reshape(1, -1)

    down_part = gather_shard(small.reshape(-1, part), 0)
    out_full = lax.all_gather(out_proj, ("shard", "ctx"), axis=1, tiled=True)
    hidden_weights = (gate_proj.T, up_proj.T, down_proj)
    if block_sized():
        pieces = hidden_pieces((after(gate_proj.T, small),) + hidden_weights[1:])
        hidden_joined = join_columns(pieces)
    else:
        gate_full, upward_full, down_full = map(hidden_rows_plain, hidden_weights)
        hidden_joined = gate_full

    up_query = gather_ctx(after(q_up, down_part))
    up_latent = gather_ctx(after(kv_up, down_part))


    heads = q_up.shape[1] // HEAD
    positions = offset + jnp.arange(piece, dtype=jnp.int32)
    cosine_here, sine_here = rope_tables(positions)
    docs = doc_lengths.shape[1]
    ends = jnp.stack([jnp.sum(doc_lengths[:, : i + 1], axis=1) for i in range(docs)], axis=1)
    starts = jnp.max(
        jnp.where(positions[None, :, None] >= ends[:, None, :], ends[:, None, :], 0), axis=-1
    )
    limits = jnp.stack([starts, jnp.broadcast_to(positions[None], starts.shape)], axis=1)
    cosine, sine = cosine_here[:, : ROPE // 2], sine_here[:, : ROPE // 2]
    zero, fill = jnp.zeros_like(cosine), jnp.zeros((piece, LANES - HEAD), f32)
    plain = jnp.zeros((piece, NOPE), f32)
    table = jnp.stack(
        [
            jnp.concatenate([plain + 1.0, cosine, cosine, fill], axis=1),
            jnp.concatenate([plain, -sine, zero, fill], axis=1),
            jnp.concatenate([plain, zero, sine, fill], axis=1),
        ]
    )

    stream = hidden_in.astype(f32).reshape(rows, width)
    grad_out = cotangent.astype(f32).reshape(rows, width)
    chunk_start = rank * chunk_rows

    def own_chunk(values):
        return lax.dynamic_slice_in_dim(values, chunk_start, chunk_rows, 0)

    inverse_one = rms_inverse(stream)
    normed_one = stream * inverse_one
    input_low = (normed_one * gain_attn).astype(bf16)
    low_rank = gather_tp(dot(input_low, down_part, ((1,), (0,))))
    up_query = gather_shard(after(up_query.reshape(-1, q_up.shape[1]), low_rank), 0)
    up_latent = gather_shard(after(up_latent.reshape(-1, kv_up.shape[1]), low_rank), 0)
    query_latent = low_rank[:, :, :q_part].transpose(1, 0, 2).reshape(rows, QRANK)
    latent_raw = low_rank[:, :, q_part:].transpose(1, 0, 2).reshape(rows, KVRANK + ROPE)
    inverse_latent = rms_inverse(latent_raw[:, :KVRANK])
    normed_latent = latent_raw[:, :KVRANK] * inverse_latent
    latent_low = (normed_latent * gain_latent).astype(bf16).reshape(seqs, piece, KVRANK)
    rotary_key = rotate(
        latent_raw[:, KVRANK:].reshape(seqs, piece, ROPE), cosine_here, sine_here
    ).astype(bf16)
    keys_here = jnp.concatenate(
        [latent_low, jnp.pad(rotary_key, ((0, 0), (0, 0), (NOPE, LANES - HEAD)))], axis=-1
    )
    half = seqs // 2
    mine = rank & 1
    keys_mine = lax.dynamic_slice_in_dim(keys_here, mine * half, half, 0)
    keys_mine = gather_ctx(after(keys_mine, hidden_joined))
    if block_sized():
        hidden_gathered = hidden_gather(after(hidden_joined, keys_mine))
        gate_full, upward_full, down_full = hidden_rows(hidden_gathered)
    keys_mine = keys_mine.transpose(1, 0, 2, 3).reshape(half, seq_len, KVRANK + LANES)
    keys_all = pair_order(keys_mine, tp_xor(keys_mine, 1), low_bit, 0)
    latent_all, rotary_all = keys_all[..., :KVRANK], keys_all[..., KVRANK:]

    grad_ffn = gather_tokens((res_scale * own_chunk(grad_out)).astype(bf16))

    inverse_query = rms_inverse(query_latent)
    normed_query = query_latent * inverse_query
    query_low = (normed_query * gain_query).astype(bf16)
    key_value = jnp.einsum("slr,rf->slf", latent_all, up_latent, preferred_element_type=f32)
    key_value = key_value.astype(bf16)
    query = dot(query_low, up_query, ((1,), (0,))).reshape(seqs, piece, -1)
    attended_low, log_total = attention_forward(
        query, key_value, rotary_all, table, limits.transpose(0, 2, 1), heads
    )
    attended_low = attended_low.reshape(rows, heads * VDIM)

    attn_out = scatter_tp(
        dot(attended_low, out_full, ((1,), (0,))).reshape(n_tp, chunk_rows, width)
    )
    middle = own_chunk(stream) + res_scale * attn_out
    inverse_two = rms_inverse(middle)
    normed_two = middle * inverse_two
    ffn_own = gather_tokens(
        (normed_two * gain_ffn).astype(bf16), *([hidden_gathered] if block_sized() else [])
    )
    ffn_groups = [ffn_own, swap(ffn_own, "tp", 1)]
    grad_ffn_groups = [grad_ffn, swap(grad_ffn, "tp", 1)]
    ffn_parts, grad_two_parts, kept = [], [], []
    for ffn_low, grad_low in zip(ffn_groups, grad_ffn_groups):
        gate_value = dot(ffn_low, gate_full, ((1,), (1,)))
        up_value = dot(ffn_low, upward_full, ((1,), (1,)))
        sigma = jax.nn.sigmoid(gate_value)
        gate_act = gate_value * sigma
        hidden_low = (gate_act * up_value).astype(bf16)
        grad_hidden = dot(grad_low, down_full, ((1,), (1,)))
        grad_gate = (grad_hidden * up_value * sigma * (1.0 + gate_value * (1.0 - sigma))).astype(
            bf16
        )
        grad_upward = (grad_hidden * gate_act).astype(bf16)
        grad_two_part = dot(grad_gate, gate_full, ((1,), (0,)))
        grad_two_part = grad_two_part + dot(grad_upward, upward_full, ((1,), (0,)))
        grad_two_parts.append(grad_two_part.astype(bf16))
        ffn_parts.append(dot(hidden_low, down_full, ((1,), (0,))).astype(bf16))
        kept.append((hidden_low.T, grad_gate.T, grad_upward.T))

    grad_two = scatter_tokens(scatter_near(*grad_two_parts))
    hidden_grads = ffn_weight_grads(
        [[group] for group in ffn_groups], [[group] for group in grad_ffn_groups], kept
    )
    if block_sized():
        hidden_sums = lax.psum_scatter(
            hidden_grads,
            "ctx",
            scatter_dimension=0,
            axis_index_groups=far_groups(),
        )
    ffn_sum = scatter_near(ffn_parts[0], after(ffn_parts[1], grad_two))
    down_all = gather_tp(after(down_part.T, grad_two)).reshape(-1, width)
    grad_middle = own_chunk(grad_out) + norm_backward(grad_two, normed_two, inverse_two, gain_ffn)
    grad_gain_ffn = jnp.sum(grad_two * normed_two, axis=0)
    grad_attn = after((res_scale * grad_middle).astype(bf16), hidden_grads)
    grad_attn = gather_tp(grad_attn).reshape(rows, width)

    grad_out_w = lax.psum_scatter(
        dot(attended_low, grad_attn, ((0,), (0,))).astype(bf16),
        ("shard", "ctx"),
        scatter_dimension=1,
        tiled=True,
    ).astype(f32)

    grad_attended = dot(grad_attn, out_full, ((1,), (1,))).astype(bf16)
    grad_query, grad_key_value, grad_krope = attention_backward(
        query,
        key_value,
        rotary_all,
        table,
        limits,
        log_total,
        grad_attended.reshape(seqs, piece, -1),
        heads,
    )
    grad_query = grad_query.reshape(rows, heads * HEAD)
    grad_key_value = grad_key_value.reshape(seqs * seq_len, heads * (NOPE + VDIM))

    grad_keys = dot(grad_key_value, up_latent, ((1,), (1,))).astype(bf16)
    grad_keys = jnp.concatenate(
        [grad_keys.reshape(seqs, seq_len, KVRANK), grad_krope.astype(bf16)], axis=-1
    )

    def add_near(values):
        keep = lax.dynamic_slice_in_dim(values, mine * half, half, 0)
        send = lax.dynamic_slice_in_dim(values, (1 - mine) * half, half, 0)
        return keep.astype(f32) + tp_xor(send, 1).astype(f32)

    grad_keys = add_near(grad_keys).astype(bf16)
    grad_keys = scatter_ctx(
        grad_keys.reshape(half, n_ctx, piece, KVRANK + LANES).transpose(1, 0, 2, 3)
    )
    grad_pre_query = dot(grad_query, up_query, ((1,), (1,))).astype(bf16)
    grad_pre_query = add_near(grad_pre_query.reshape(seqs, piece, QRANK))
    ffn_sum = scatter_step(scatter_begin(ffn_sum), 2)
    grad_low = jnp.concatenate([grad_pre_query, grad_keys], axis=-1).astype(bf16)
    grad_low = after(grad_low, *ffn_sum)
    grad_low = (grad_low.astype(f32) + tp_xor(grad_low, 2).astype(f32)).astype(bf16)
    grad_low = pair_order(grad_low, tp_xor(grad_low, 1), low_bit, 0)
    ffn_sum = scatter_step(ffn_sum, 1)
    grad_low = after(grad_low.reshape(rows, QRANK + KVRANK + LANES), *ffn_sum)
    ffn_sum = scatter_end(scatter_step(ffn_sum, 0))
    hidden_back = []
    if block_sized():
        hidden_back = exchange_group(split_columns(hidden_sums))
        down_all = after(down_all, *hidden_back)
    grad_low = grad_low.astype(f32)

    grad_out_query, grad_out_latent = grad_low[:, :QRANK], grad_low[:, QRANK : QRANK + KVRANK]
    grad_query_latent = norm_backward(grad_out_query, normed_query, inverse_query, gain_query)
    grad_compressed = norm_backward(grad_out_latent, normed_latent, inverse_latent, gain_latent)
    grad_gain_query = jnp.sum(own_chunk(grad_out_query * normed_query), axis=0)
    grad_gain_latent = jnp.sum(own_chunk(grad_out_latent * normed_latent), axis=0)
    grad_rotary = grad_low[:, QRANK + KVRANK + NOPE : QRANK + KVRANK + HEAD]
    grad_rotary = grad_rotary.reshape(seqs, piece, ROPE)
    grad_rotary = unrotate(grad_rotary, cosine_here, sine_here).reshape(rows, ROPE)
    grad_query_latent = grad_query_latent.astype(bf16)
    grad_latent_raw = jnp.concatenate([grad_compressed, grad_rotary], axis=-1).astype(bf16)

    own_query, own_latent = own_chunk(grad_query_latent), own_chunk(grad_latent_raw)
    grad_parts = [
        part_of[:, i * length : (i + 1) * length]
        for i in range(n_tp)
        for part_of, length in ((own_query, q_part), (own_latent, kv_part))
    ]
    grad_pre_one = dot(jnp.concatenate(grad_parts, axis=1), down_all, ((1,), (0,)))
    normed_own = own_chunk(normed_one)
    grad_input = grad_middle + norm_backward(
        grad_pre_one, normed_own, own_chunk(inverse_one), gain_attn
    )
    grad_gain_attn = jnp.sum(grad_pre_one * normed_own, axis=0)
    grad_input = round_low(grad_input).astype(bf16)
    grad_input = gather_tp(grad_input).astype(f32)

    grad_part = jnp.concatenate(
        [
            lax.dynamic_slice_in_dim(grad_query_latent, rank * q_part, q_part, 1),
            lax.dynamic_slice_in_dim(grad_latent_raw, rank * kv_part, kv_part, 1),
        ],
        axis=1,
    )
    grad_small = dot(input_low, grad_part, ((0,), (0,)))
    grad_half = scatter_shard(grad_small, 0)
    grad_small = scatter_ctx(grad_half.reshape(n_ctx, n_tp, block, part))
    grad_small = exchange_tp(grad_small.astype(bf16)).astype(f32).transpose(1, 0, 2)
    grad_down_query = grad_small[:, :, :q_part].reshape(block, QRANK)
    grad_down_latent = grad_small[:, :, q_part:].reshape(block, KVRANK + ROPE)
    grad_gains = jnp.concatenate(
        [
            grad_gain_attn.reshape(n_blocks, -1),
            grad_gain_ffn.reshape(n_blocks, -1),
            grad_gain_query.reshape(n_blocks, -1),
            grad_gain_latent.reshape(n_blocks, -1),
        ],
        axis=1,
    )
    grad_gains = lax.all_to_all(grad_gains[:, None], everywhere, 0, 0)
    grad_gains = jnp.sum(grad_gains[:, 0], axis=0)

    output = round_low(middle + res_scale * ffn_sum)
    output = gather_tp(output.astype(bf16)).astype(f32)

    def rows_grad(grad):
        mine = scatter_shard(grad, 0)
        return scatter_ctx(mine.reshape(n_ctx, -1, mine.shape[-1]))

    grad_up_query = rows_grad(dot(query_low, grad_query, ((0,), (0,))))
    grad_up_latent = rows_grad(
        dot(latent_all.reshape(-1, KVRANK), grad_key_value, ((0,), (0,)))
    )
    if block_sized():
        grad_gate_w, grad_upward_w, grad_down_w = place_rows(hidden_back)
    else:
        units = hidden_grads.shape[1] // 3
        split = [hidden_grads[:, i * units : (i + 1) * units] for i in range(3)]
        grad_gate_w, grad_upward_w, grad_down_w = map(hidden_grad_plain, split)
        grad_gate_w, grad_upward_w = grad_gate_w.T, grad_upward_w.T
    return (
        output.reshape(seqs, piece, width),
        grad_input.reshape(seqs, piece, width),
        grad_gains[:cut],
        grad_gains[2 * cut : 2 * cut + q_gain.shape[0]],
        grad_gains[2 * cut + q_gain.shape[0] :],
        grad_gains[cut : 2 * cut],
        grad_down_query,
        grad_down_latent,
        grad_up_query,
        grad_up_latent,
        grad_out_w,
        grad_gate_w,
        grad_upward_w,
        grad_down_w,
    )


def solution(mesh):
    all_axes = ("shard", "ctx", "tp")
    tokens, vector, square = P("shard", "ctx", None), P(all_axes), P(all_axes, None)
    inner, outer = P(("shard", "ctx"), "tp"), P("tp", ("shard", "ctx"))
    weights = (
        vector,
        vector,
        vector,
        vector,
        square,
        square,
        inner,
        inner,
        outer,
        inner,
        inner,
        outer,
    )
    return jax.shard_map(
        on_device,
        mesh=mesh,
        in_specs=(tokens, tokens, P("shard", None)) + weights,
        out_specs=(tokens, tokens) + weights,
        check_vma=False,
    )
```
